128 devices in a mesh: expert: 16 (over z, y), tensor: 8 (over x, core).
Axes of the slice: x: 4, y: 4, z: 4, core: 2. Of those that a mesh axis runs over, the one named last changes fastest.
Arguments:
- tokens: bfloat16 [2048, 4096], P('expert'), may hold values from -6 to 6
- expert_ids: int32 [2048, 8], P('expert'), may hold values from 0 to 31, all different within a row; in each aligned block of 128 rows (0 to 127, 128 to 255, ...) at most 48 rows name the same one
- route_weights: float32 [2048, 8], P('expert'), may hold values from 0.1 to 0.5
- grad_out: bfloat16 [2048, 4096], P('expert'), may hold values from -6 to 6
- w_gate: bfloat16 [32, 1536, 4096], P('expert', 'tensor'), may hold values from -0.09375 to 0.09375
- w_up: bfloat16 [32, 1536, 4096], P('expert', 'tensor'), may hold values from -0.09375 to 0.09375
- w_down: bfloat16 [32, 1536, 4096], P('expert', 'tensor'), may hold values from -0.15625 to 0.15625
Outputs:
- grad_tokens: bfloat16 [2048, 4096], P('expert', 'tensor')
- grad_gate: bfloat16 [32, 1536, 4096], P('expert', 'tensor')
- grad_up: bfloat16 [32, 1536, 4096], P('expert', 'tensor')
- grad_down: bfloat16 [32, 1536, 4096], P('expert', 'tensor')
The draws below stay inside these ranges and needn't reach their ends.
Inputs may be any that keep to these rules, and one draw needn't show every extreme that they name: `expert_ids`: each row names 8 different experts. Among the 128 rows of one block (aligned blocks of rows, one a device of the expert axis) no expert is named by more than 48 rows, and in every draw some expert is named by exactly 48 rows of some block.
All inputs are finite; a program needn't handle non-finite values.
Results may differ from the reference program's by a relative error of at most 0.02.
Values may be sent and summed in bfloat16 or wider, within the bound.
No kernel may reach another device: no remote copies, remote signals or barrier semaphores. Data moves between devices by JAX's collectives and lax.ppermute only.
A program may use at most 192 MiB of HBM per device.

```python
import math
import jax
import jax.numpy as jnp
import numpy as np
from jax import lax

D = 4096
FF = 1536
TOP = 8
TOK_DEV = 128
EXPERTS = 32
CAP = 48
TOKENS = 2048
N_EXPERT = 16
N_TENSOR = 8


def block_scale(key, extent, shards, smallest, top_value):
    def one(dim, parts):
        draws = jax.random.uniform(jax.random.fold_in(jax.random.fold_in(key, 6), dim), (parts,), jnp.float32, smallest / len(shards), top_value / len(shards))
        return jnp.repeat(jnp.exp(draws), extent[dim] // parts).reshape((-1,) + (1,) * (len(extent) - dim - 1))

    loudness = one(*shards[0])
    for cut in shards[1:]:
        loudness = loudness * one(*cut)
    return loudness


def deal_out(own_key, own, number, rows, count, top, most, slope):
    ranking = jax.random.permutation(own_key, count)
    crowded, common = shares(count, rows * top, most, slope, True), shares(count, rows * top, most, slope, False)
    places = jnp.arange(count)

    def named(sizes, rotation):
        used = int((sizes > 0).sum())
        fixed = max(1, used // 4)
        moved = fixed + (places - fixed + rotation * (used - fixed)) % max(1, count - fixed)
        return jnp.zeros((count,), jnp.int32).at[ranking[jnp.where(places < fixed, places, moved)]].set(jnp.asarray(sizes, jnp.int32))

    sizes = jnp.where(number % 4 == 0, named(crowded, number // 4), named(common, number - number // 4 - 1))
    mixed = jax.random.permutation(jax.random.fold_in(own, 3), count)
    donor, receiver = mixed[0:count // 2 * 2:2], mixed[1:count // 2 * 2:2]
    room = jnp.minimum(sizes[donor] - 1, most - sizes[receiver]) // 2
    room = jnp.where((donor == ranking[0]) | (receiver == ranking[0]) | (sizes[receiver] == 0), 0, jnp.maximum(room, 0))
    moved = jax.random.randint(jax.random.fold_in(own, 4), (count // 2,), 0, 1 << 20) % (room + 1)
    sizes = sizes.at[donor].add(-moved).at[receiver].add(moved)
    members = jnp.searchsorted(jnp.cumsum(sizes), jnp.arange(rows * top), side="right").astype(jnp.int32)
    listing = members.reshape(top, rows).T
    listing = listing[jax.random.permutation(jax.random.fold_in(own, 1), rows)]
    rotation = jax.random.randint(jax.random.fold_in(own, 2), (rows, 1), 0, top)
    return jnp.take_along_axis(listing, (jnp.arange(top)[None, :] + rotation) % top, axis=1)


def shares(number_of, total, bound, skew, full):
    weights = [(1 << 20) // math.isqrt(standing ** skew) + 1 for standing in range(1, number_of + 1)]
    largest = bound if full else min(bound, max(-(-total // number_of), total * weights[0] // sum(weights)))
    least = 1 if total - largest >= number_of - 1 else 0
    holding, surplus = [largest] + [least] * (number_of - 1), total - largest - least * (number_of - 1)
    while surplus > 0:
        movable = [i for i in range(1, number_of) if holding[i] < largest] or [i for i in range(1, number_of) if holding[i] < bound]
        mass, remaining = sum([weights[i] for i in movable]), surplus
        for i in movable:
            more = min(bound - holding[i], max(1, remaining * weights[i] // mass), surplus)
            holding[i] = holding[i] + more
            surplus = surplus - more
    return np.array(holding)


def gaussian(own_key, extent, scale, limit, pieces=(), held_as=jnp.bfloat16):
    values = scale * jax.random.normal(own_key, extent, jnp.float32)
    if pieces:
        values = values * block_scale(own_key, extent, pieces, -0.22, 0.18)
    return jnp.clip(values, -limit, limit).astype(held_as)


def setup_inputs(seed: int = 0) -> dict:
    splits = jax.random.split(jax.random.key(seed), 8)
    tokens = gaussian(splits[0], (TOKENS, D), 1.0, 6.0, ((0, 16),))
    expert_ids_keys = jax.random.split(jax.random.fold_in(splits[1], 1), TOKENS // TOK_DEV)
    expert_ids_turns = jax.random.permutation(jax.random.fold_in(splits[1], 3), TOKENS // TOK_DEV)
    expert_ids = jax.vmap(lambda own, number: deal_out(jax.random.fold_in(splits[1], 2), own, number, TOK_DEV, EXPERTS, TOP, CAP, 2))(expert_ids_keys, expert_ids_turns).reshape((TOKENS, TOP))
    route_weights = jnp.clip(0.1 + 0.4 * jax.random.uniform(splits[2], (TOKENS, TOP), jnp.float32) ** block_scale(splits[2], (TOKENS, TOP), ((0, 16),), -0.2, 0.2), 0.1, 0.5)
    grad_out = gaussian(splits[3], (TOKENS, D), 1.0, 6.0, ((0, 16),))
    w_gate = gaussian(splits[4], (EXPERTS, FF, D), D ** -0.5, 0.09375, ((0, 16), (1, 8)))
    w_up = gaussian(splits[5], (EXPERTS, FF, D), D ** -0.5, 0.09375, ((0, 16), (1, 8)))
    w_down = gaussian(splits[6], (EXPERTS, FF, D), FF ** -0.5, 0.15625, ((0, 16), (1, 8)))
    return {"tokens": tokens, "expert_ids": expert_ids, "route_weights": route_weights, "grad_out": grad_out, "w_gate": w_gate, "w_up": w_up, "w_down": w_down}


def slot_numbers(id_block, experts, cap):
    flat = id_block.reshape(-1).astype(jnp.int32)
    onehot = (flat[:, None] == jnp.arange(experts, dtype=jnp.int32)[None, :]).astype(jnp.int32)
    before = jnp.cumsum(onehot, axis=0) - onehot
    position = jnp.sum(before * onehot, axis=1).astype(jnp.int32)
    return flat * cap + position


def reference(tokens, expert_ids, route_weights, grad_out, w_gate, w_up, w_down):
    blocks = expert_ids.reshape(N_EXPERT, TOK_DEV, TOP)
    local = jax.vmap(lambda one_block: slot_numbers(one_block, EXPERTS, CAP))(blocks)
    block_number = jnp.arange(N_EXPERT, dtype=jnp.int32)[:, None]
    slot_list = ((local // CAP) * (N_EXPERT * CAP) + block_number * CAP + local % CAP).reshape(-1).astype(jnp.int32)
    pair_count = TOKENS * TOP
    owner = jnp.full((EXPERTS * N_EXPERT * CAP,), pair_count, jnp.int32)
    owner = owner.at[slot_list].set(jnp.arange(pair_count, dtype=jnp.int32))
    token_index = owner // TOP
    token_pad = jnp.concatenate([tokens, jnp.zeros((1, D), jnp.bfloat16)], axis=0)
    grad_pad = jnp.concatenate([grad_out, jnp.zeros((1, D), jnp.bfloat16)], axis=0)
    weight_pad = jnp.concatenate([route_weights.reshape(-1), jnp.zeros((1,), jnp.float32)], axis=0)
    rows_each = N_EXPERT * CAP
    x_slots = token_pad[token_index].reshape(EXPERTS, rows_each, D)
    g_slots = (weight_pad[owner][:, None] * grad_pad[token_index].astype(jnp.float32)).astype(jnp.bfloat16)
    g_slots = g_slots.reshape(EXPERTS, rows_each, D)
    width = FF // N_TENSOR

    def expert_step(operands):
        x_rows, g_rows, gate_w, up_w, down_w = operands
        gate_pre = jnp.dot(x_rows, gate_w.T, preferred_element_type=jnp.float32)
        up_pre = jnp.dot(x_rows, up_w.T, preferred_element_type=jnp.float32)
        sigmoid_gate = jax.nn.sigmoid(gate_pre)
        silu_gate = gate_pre * sigmoid_gate
        act = (silu_gate * up_pre).astype(jnp.bfloat16)
        d_hidden = jnp.dot(g_rows, down_w.T, preferred_element_type=jnp.float32)
        d_gate = (d_hidden * up_pre * sigmoid_gate * (1.0 + gate_pre * (1.0 - sigmoid_gate))).astype(jnp.bfloat16)
        d_up = (d_hidden * silu_gate).astype(jnp.bfloat16)
        grad_down = jnp.dot(act.T, g_rows, preferred_element_type=jnp.float32).astype(jnp.bfloat16)
        grad_gate = jnp.dot(d_gate.T, x_rows, preferred_element_type=jnp.float32).astype(jnp.bfloat16)
        grad_up = jnp.dot(d_up.T, x_rows, preferred_element_type=jnp.float32).astype(jnp.bfloat16)
        total = jnp.zeros((rows_each, D), jnp.float32)
        for block in range(N_TENSOR):
            low = block * width
            partial_value = jnp.dot(d_gate[:, low:low + width], gate_w[low:low + width, :], preferred_element_type=jnp.float32)
            partial_value = partial_value + jnp.dot(d_up[:, low:low + width], up_w[low:low + width, :], preferred_element_type=jnp.float32)
            total = total + lax.optimization_barrier(partial_value.astype(jnp.bfloat16)).astype(jnp.float32)
        return grad_gate, grad_up, grad_down, total.astype(jnp.bfloat16)

    grad_gate, grad_up, grad_down, slot_grad = lax.map(expert_step, (x_slots, g_slots, w_gate, w_up, w_down))
    slot_flat = slot_grad.reshape(EXPERTS * rows_each, D)
    picked = slot_flat[slot_list].astype(jnp.float32).reshape(TOKENS, TOP, D)
    grad_tokens = jnp.sum(picked, axis=1).astype(jnp.bfloat16)
    return grad_tokens, grad_gate, grad_up, grad_down
```

```python
import jax
import jax.numpy as jnp
from jax import lax
from jax.experimental import pallas as pl
from jax.experimental.pallas import tpu as pltpu
from jax.sharding import Mesh
from jax.sharding import PartitionSpec as P

BF = jnp.bfloat16
F32 = jnp.float32
CAP = 48
ZY = ("z", "y")
VMEM = pl.BlockSpec(memory_space=pltpu.VMEM)
SMEM = pl.BlockSpec(memory_space=pltpu.SMEM)
SWAP = [(0, 1), (1, 0)]


def params(mib):
    return pltpu.CompilerParams(vmem_limit_bytes=mib * 1024 * 1024)


def cost(flops, nbytes):
    return pl.CostEstimate(flops=int(flops), bytes_accessed=int(nbytes), transcendentals=0)


def nt(a, b):
    return lax.dot_general(a, b, (((1,), (1,)), ((), ())), preferred_element_type=F32)


def tn(a, b):
    return lax.dot_general(a, b, (((0,), (0,)), ((), ())), preferred_element_type=F32)


def places_kernel(c_ref, ids_ref, wts_ref, out_ref):
    rows, top = ids_ref.shape
    lane = lax.broadcasted_iota(jnp.int32, (rows, 128), 1)
    expert = 2 * lane + c_ref[0]
    hit = jnp.zeros((rows, 128), F32)
    wt = jnp.zeros((rows, 128), F32)
    for k in range(top):
        same = ids_ref[:, k : k + 1] == expert
        hit = hit + same.astype(F32)
        wt = wt + jnp.where(same, wts_ref[:, k : k + 1], 0.0)
    r = lax.broadcasted_iota(jnp.int32, (rows, rows), 0)
    q = lax.broadcasted_iota(jnp.int32, (rows, rows), 1)
    before = jnp.dot((q < r).astype(BF), hit.astype(BF), preferred_element_type=F32)
    pos = jnp.where(hit > 0.5, before, -1.0)
    out_ref[:, 0:rows] = pos.T[0:16, :]
    out_ref[:, rows : 2 * rows] = wt.T[0:16, :]


def chosen(row, count):
    p = lax.broadcasted_iota(jnp.int32, (CAP, count), 0).astype(F32)
    return row == p


def forward_kernel(pw_ref, ag_ref, wgu_ref, wd_ref, xo_ref, go_ref, act_ref, dgu_ref, xs, gs, pre, dh):
    step = pl.program_id(0)
    hidden = wd_ref.shape[0]
    picks, scales = [], []
    for i in range(2):
        row = pw_ref[pl.ds(2 * step + i, 1), :]
        pick = chosen(row[:, 0:128], 128)
        scales.append(jnp.sum(jnp.where(pick, row[:, 128:256], 0.0), axis=1, keepdims=True))
        wide = pick.astype(F32)
        none = jnp.zeros((CAP, 128), F32)
        picks.append(jnp.concatenate([wide, none] if i == 0 else [none, wide], axis=1))
    pick = jnp.concatenate(picks, axis=0).astype(BF)
    scale = jnp.concatenate(scales, axis=0)
    at = pl.ds(pl.multiple_of(step * 2 * CAP, 2 * CAP), 2 * CAP)
    for t in range(8):
        both = jnp.concatenate([ag_ref[t], ag_ref[8 + t]], axis=0)
        got = jnp.dot(pick, both, preferred_element_type=F32)
        x = got[:, 0:512].astype(BF)
        g = (got[:, 512:1024] * scale).astype(BF)
        cols = slice(t * 512, (t + 1) * 512)
        xs[at, cols] = x
        gs[at, cols] = g
        xo_ref[:, cols] = x
        go_ref[:, cols] = g

    @pl.when(step % 4 == 3)
    def _():
        rows = pl.ds(pl.multiple_of((step // 4) * 8 * CAP, 8 * CAP), 8 * CAP)

        @pl.loop(0, 3)
        def _(n):
            pre[n] = nt(xs[rows, :], wgu_ref[pl.ds(pl.multiple_of(n * 256, 256), 256), :])

        dh[...] = nt(gs[rows, :], wd_ref[...])
        both = jnp.concatenate([pre[0], pre[1], pre[2]], axis=1)
        gate, up = both[:, 0:hidden], both[:, hidden : 2 * hidden]
        sig = jax.nn.sigmoid(gate)
        silu = gate * sig
        d = dh[...]
        act_ref[rows, :] = (silu * up).astype(BF)
        dgu_ref[rows, 0:hidden] = (d * up * sig * (1.0 + gate * (1.0 - sig))).astype(BF)
        dgu_ref[rows, hidden : 2 * hidden] = (d * silu).astype(BF)


def partial_kernel(dgu_ref, wgu_ref, out_ref):
    out_ref[0] = jnp.dot(dgu_ref[...], wgu_ref[...], preferred_element_type=F32).astype(BF)


def weight_kernel(c_ref, dgu_ref, act_ref, xs_ref, gs_ref, gg_ref, gu_ref, gd_ref, sg_ref, su_ref, sd_ref, dt, at):
    f = gg_ref.shape[1]

    @pl.when(pl.program_id(0) == 0)
    def _():
        dt[...] = dgu_ref[...].astype(F32).T.astype(BF)
        at[...] = act_ref[...].astype(F32).T.astype(BF)

    gu = jnp.dot(dt[...], xs_ref[...], preferred_element_type=F32).astype(BF)
    gd = jnp.dot(at[...], gs_ref[...], preferred_element_type=F32).astype(BF)
    gg_ref[0] = gu[0:f]
    sg_ref[...] = gu[f : 2 * f]
    gu_ref[0] = gu[2 * f : 3 * f]
    su_ref[...] = gu[3 * f : 4 * f]
    gd_ref[0] = gd[0:f]
    sd_ref[...] = gd[f : 2 * f]


def combine_kernel(c_ref, pw_ref, ret_ref, keep_ref, send_ref):
    picks = [chosen(pw_ref[e : e + 1, 0:128], 128).astype(F32) for e in range(16)]
    pick = jnp.concatenate(picks, axis=0).T.astype(BF)
    total = jnp.dot(pick, ret_ref[...], preferred_element_type=F32)
    low = c_ref[0] == 0
    left, right = total[:, 0:512], total[:, 512:1024]
    keep_ref[...] = jnp.where(low, left, right)
    send_ref[...] = jnp.where(low, right, left)


def swap(v):
    return lax.ppermute(v, "c", SWAP)


def shards(tokens, expert_ids, route_weights, grad_out, w_gate, w_up, w_down):
    rows, width = tokens.shape
    f = w_gate.shape[1]
    slots = 16 * CAP
    c = lax.axis_index("c")
    t = lax.axis_index("x") * 2 + c
    cs = jnp.reshape(c, (1,)).astype(jnp.int32)

    own = jnp.concatenate(
        [lax.dynamic_slice_in_dim(v, t * 512, 512, 1) for v in (tokens, grad_out)], axis=1
    )
    gathered = lax.all_gather(own, ("z", "y", "x", "c"), axis=0, tiled=False)

    pw_own = pl.pallas_call(
        places_kernel,
        out_shape=jax.ShapeDtypeStruct((16, 2 * rows), F32),
        in_specs=[SMEM, VMEM, VMEM],
        out_specs=VMEM,
        name="places",
    )(cs, expert_ids, route_weights)
    pw = lax.all_to_all(pw_own, ZY, split_axis=0, concat_axis=0, tiled=True)

    mine = [lax.dynamic_index_in_dim(w, c, 0, False) for w in (w_gate, w_up, w_down)]
    other = [swap(lax.dynamic_index_in_dim(w, 1 - c, 0, False)) for w in (w_gate, w_up, w_down)]
    wgu = jnp.concatenate([mine[0], other[0], mine[1], other[1]], axis=0)
    wd = jnp.concatenate([mine[2], other[2]], axis=0)

    xs, gs, act, dgu = pl.pallas_call(
        forward_kernel,
        grid=(8,),
        out_shape=(
            jax.ShapeDtypeStruct((slots, width), BF),
            jax.ShapeDtypeStruct((slots, width), BF),
            jax.ShapeDtypeStruct((slots, 2 * f), BF),
            jax.ShapeDtypeStruct((slots, 4 * f), BF),
        ),
        in_specs=[VMEM, pl.BlockSpec((16, rows, 1024), lambda b: (b, 0, 0)), VMEM, VMEM],
        out_specs=(
            pl.BlockSpec((2 * CAP, width), lambda b: (b, 0)),
            pl.BlockSpec((2 * CAP, width), lambda b: (b, 0)),
            VMEM,
            VMEM,
        ),
        scratch_shapes=[
            pltpu.VMEM((slots, width), BF),
            pltpu.VMEM((slots, width), BF),
            pltpu.VMEM((3, 8 * CAP, 256), F32),
            pltpu.VMEM((8 * CAP, 2 * f), F32),
        ],
        compiler_params=params(56),
        cost_estimate=cost(2 * slots * width * 6 * f, 60e6),
        name="forward",
    )(pw, gathered, wgu, wd)

    partial_value = pl.pallas_call(
        partial_kernel,
        grid=(8,),
        out_shape=jax.ShapeDtypeStruct((4, slots, 1024), BF),
        in_specs=[VMEM, pl.BlockSpec((4 * f, 512), lambda j: (0, j))],
        out_specs=pl.BlockSpec((1, slots, 512), lambda j: (j // 2, 0, j % 2)),
        compiler_params=params(32),
        cost_estimate=cost(2 * slots * width * 4 * f, 14e6),
        name="partial",
    )(dgu, wgu)
    summed = lax.psum_scatter(
        partial_value.reshape(4 * slots, 1024), "x", scatter_dimension=0, tiled=True
    )

    whole = jax.ShapeDtypeStruct((2, f, width), BF)
    piece = jax.ShapeDtypeStruct((f, width), BF)
    gg, gu, gd, sg, su, sd = pl.pallas_call(
        weight_kernel,
        grid_spec=pltpu.PrefetchScalarGridSpec(
            num_scalar_prefetch=1,
            grid=(8,),
            in_specs=[
                VMEM,
                VMEM,
                pl.BlockSpec((slots, 512), lambda j, cr: (0, j)),
                pl.BlockSpec((slots, 512), lambda j, cr: (0, j)),
            ],
            out_specs=[pl.BlockSpec((1, f, 512), lambda j, cr: (cr[0], 0, j))] * 3
            + [pl.BlockSpec((f, 512), lambda j, cr: (0, j))] * 3,
            scratch_shapes=[pltpu.VMEM((4 * f, slots), BF), pltpu.VMEM((2 * f, slots), BF)],
        ),
        out_shape=[whole] * 3 + [piece] * 3,
        compiler_params=params(40),
        cost_estimate=cost(2 * slots * width * 6 * f, 24e6),
        name="weights",
    )(cs, dgu, act, xs, gs)
    grads = [
        lax.dynamic_update_index_in_dim(g, swap(s), 1 - c, 0)
        for g, s in ((gg, sg), (gu, su), (gd, sd))
    ]

    returned = lax.all_to_all(summed, ZY, split_axis=0, concat_axis=0, tiled=True)
    half = jax.ShapeDtypeStruct((rows, 512), F32)
    keep, send = pl.pallas_call(
        combine_kernel,
        out_shape=(half, half),
        in_specs=[SMEM, VMEM, VMEM],
        out_specs=(VMEM, VMEM),
        compiler_params=params(32),
        name="combine",
    )(cs, pw_own, returned)
    grad_tokens = (keep + swap(send)).astype(BF)
    return (grad_tokens, *grads)


def solution(mesh):
    fine = Mesh(mesh.devices.reshape(4, 4, 4, 2), ("z", "y", "x", "c"))
    rows = P(ZY, None)
    weights = P(ZY, ("x", "c"), None)
    return jax.shard_map(
        shards,
        mesh=fine,
        in_specs=(rows, rows, rows, rows, weights, weights, weights),
        out_specs=(P(ZY, ("x", "c")), weights, weights, weights),
        check_vma=False,
    )
```

```python
import jax
import jax.numpy as jnp
from jax import lax
from jax.experimental import pallas as pl
from jax.experimental.pallas import tpu as pltpu
from jax.sharding import Mesh
from jax.sharding import PartitionSpec as P

BF = jnp.bfloat16
F32 = jnp.float32
CAP = 48
ZY = ("z", "y")
ZYX = ("z", "y", "x")
VMEM = pl.BlockSpec(memory_space=pltpu.VMEM)
SMEM = pl.BlockSpec(memory_space=pltpu.SMEM)
SWAP = [(0, 1), (1, 0)]


def params(mib):
    return pltpu.CompilerParams(vmem_limit_bytes=mib * 1024 * 1024)


def cost(flops, nbytes):
    return pl.CostEstimate(flops=int(flops), bytes_accessed=int(nbytes), transcendentals=0)


def nt(a, b):
    return lax.dot_general(a, b, (((1,), (1,)), ((), ())), preferred_element_type=F32)


def mm(a, b):
    return jnp.dot(a, b, preferred_element_type=F32)


def swap(v):
    return lax.ppermute(v, "c", SWAP)


def like(shape, dtype=BF):
    return jax.ShapeDtypeStruct(shape, dtype)


def prefetched(grid, in_specs, out_specs, scratch=()):
    return pltpu.PrefetchScalarGridSpec(
        num_scalar_prefetch=1, grid=grid, in_specs=in_specs, out_specs=out_specs, scratch_shapes=list(scratch)
    )


def places_kernel(ids_ref, wts_ref, out_ref):
    rows, top = ids_ref.shape
    lane = lax.broadcasted_iota(jnp.int32, (rows, 128), 1)
    hit = jnp.zeros((rows, 128), F32)
    wt = jnp.zeros((rows, 128), F32)
    for k in range(top):
        same = ids_ref[:, k : k + 1] == lane
        hit = hit + same.astype(F32)
        wt = wt + jnp.where(same, wts_ref[:, k : k + 1], 0.0)
    r = lax.broadcasted_iota(jnp.int32, (rows, rows), 0)
    q = lax.broadcasted_iota(jnp.int32, (rows, rows), 1)
    before = mm((q < r).astype(BF), hit.astype(BF))
    pos = jnp.where(hit > 0.5, before, -1.0)
    out_ref[:, 0:rows] = pos.T[0:32, :]
    out_ref[:, rows : 2 * rows] = wt.T[0:32, :]


def chosen(row):
    p = lax.broadcasted_iota(jnp.int32, (CAP, row.shape[1]), 0).astype(F32)
    return row == p


def outgoing_kernel(c_ref, g_ref, u_ref, d_ref, out_ref):
    out_ref[0:2] = g_ref[...]
    out_ref[2:4] = u_ref[...]
    out_ref[4:6] = d_ref[...]


def assemble_kernel(c_ref, g_ref, u_ref, d_ref, in_ref, wgu_ref, wd_ref):
    f = g_ref.shape[1]

    def place(low, high):
        for e in range(2):
            wgu_ref[e, low : low + f] = g_ref[e]
            wgu_ref[e, high : high + f] = in_ref[e]
            wgu_ref[e, 2 * f + low : 3 * f + low] = u_ref[e]
            wgu_ref[e, 2 * f + high : 3 * f + high] = in_ref[2 + e]
            wd_ref[e, low : low + f] = d_ref[e]
            wd_ref[e, high : high + f] = in_ref[4 + e]

    @pl.when(c_ref[0] == 0)
    def _():
        place(0, f)

    @pl.when(c_ref[0] == 1)
    def _():
        place(f, 0)


def select_kernel(pw_ref, ag_ref, xs_ref, gs_ref):
    step = pl.program_id(0)
    none = jnp.zeros((CAP, 128), F32)
    picks, scales = [], []
    for e in range(2):
        for i in range(2):
            row = pw_ref[pl.ds(4 * step + 2 * i + e, 1), :]
            pick = chosen(row[:, 0:128])
            scales.append(jnp.sum(jnp.where(pick, row[:, 128:256], 0.0), axis=1, keepdims=True))
            wide = pick.astype(F32)
            picks.append(jnp.concatenate([wide, none] if i == 0 else [none, wide], axis=1))
    pick = jnp.concatenate(picks, axis=0).astype(BF)
    scale = jnp.concatenate(scales, axis=0)
    for x in range(4):
        both = jnp.concatenate([ag_ref[x], ag_ref[4 + x]], axis=0)
        got = mm(pick, both)
        cols = slice(x * 512, (x + 1) * 512)
        xv = got[:, 0:512].astype(BF)
        gv = (got[:, 512:1024] * scale).astype(BF)
        for e in range(2):
            xs_ref[e, :, cols] = xv[e * 2 * CAP : (e + 1) * 2 * CAP]
            gs_ref[e, :, cols] = gv[e * 2 * CAP : (e + 1) * 2 * CAP]


def hidden_kernel(e_ref, xs_ref, gs_ref, wgu_ref, wd_ref, out_ref):
    n = wgu_ref.shape[1]
    a = nt(xs_ref[0], wgu_ref[0])
    b = nt(gs_ref[0], wd_ref[0])

    @pl.when(pl.program_id(0) == 0)
    def _():
        out_ref[:, 0:n] = a
        out_ref[:, n:] = b

    @pl.when(pl.program_id(0) > 0)
    def _():
        out_ref[:, 0:n] += a
        out_ref[:, n:] += b


def act_kernel(h_ref, r_ref, out_ref):
    n = out_ref.shape[1] // 3
    h = h_ref[...] + r_ref[...]
    gate, up, d = h[:, 0:n], h[:, n : 2 * n], h[:, 2 * n :]
    sig = jax.nn.sigmoid(gate)
    silu = gate * sig
    out_ref[:, 0:n] = (d * up * sig * (1.0 + gate * (1.0 - sig))).astype(BF)
    out_ref[:, n : 2 * n] = (d * silu).astype(BF)
    out_ref[:, 2 * n :] = (silu * up).astype(BF)


def partial_kernel(e_ref, ad_ref, wgu_ref, *rest):
    out_ref = rest[-1]
    n = wgu_ref.shape[1]
    got = mm(ad_ref[:, 0:n], wgu_ref[0]).astype(BF)
    out_ref[:, 0, 0] = got.reshape(16, CAP, 512)


def weight_kernel(c_ref, mine_ref, theirs_ref, xs_ref, gs_ref, gg_ref, gu_ref, gd_ref, send_ref, dt):
    f = gg_ref.shape[1]
    first = pl.program_id(1) == 0

    @pl.when(first & (pl.program_id(0) == 0))
    def _():
        dt[...] = mine_ref[...].astype(F32).T.astype(BF)

    @pl.when(first & (pl.program_id(0) == 1))
    def _():
        dt[...] = theirs_ref[...].astype(F32).T.astype(BF)

    c = c_ref[0]
    outs = (gg_ref, gu_ref, gd_ref)
    for i in range(3):
        rows = xs_ref if i < 2 else gs_ref
        keep = pl.ds(pl.multiple_of(2 * f * i + f * c, f), f)
        away = pl.ds(pl.multiple_of(2 * f * i + f * (1 - c), f), f)
        outs[i][0] = mm(dt[keep, :], rows[0]).astype(BF)
        send_ref[0, i] = mm(dt[away, :], rows[0]).astype(BF)


def settle_kernel(c_ref, in_ref, a_ref, b_ref, d_ref, gg_ref, gu_ref, gd_ref):
    for e in range(2):
        gg_ref[e] = in_ref[e, 0]
        gu_ref[e] = in_ref[e, 1]
        gd_ref[e] = in_ref[e, 2]


def combine_kernel(c_ref, pw_ref, ret_ref, out_ref):
    low = c_ref[0] == 0
    picks = []
    for e in range(16):
        a, b = pw_ref[2 * e : 2 * e + 1, 0:128], pw_ref[2 * e + 1 : 2 * e + 2, 0:128]
        picks.append(chosen(jnp.where(low, a, b)).astype(F32))
        picks.append(chosen(jnp.where(low, b, a)).astype(F32))
    pick = jnp.concatenate(picks, axis=0).T.astype(BF)
    total = mm(pick, ret_ref[:, 0].reshape(32 * CAP, 512))
    for x in range(1, 4):
        total = total + mm(pick, ret_ref[:, x].reshape(32 * CAP, 512))
    out_ref[...] = total.astype(BF)


def shards(tokens, expert_ids, route_weights, grad_out, w_gate, w_up, w_down):
    rows, width = tokens.shape
    f = w_gate.shape[1]
    slots = 16 * CAP
    half = width // 2
    c = lax.axis_index("c")
    x = lax.axis_index("x")
    cs = jnp.reshape(c, (1,)).astype(jnp.int32)
    others = 1 - cs

    at = x * 1024 + c * 512
    own = jnp.concatenate([lax.dynamic_slice_in_dim(v, at, 512, 1) for v in (tokens, grad_out)], axis=1)
    gathered = lax.all_gather(own, ZYX, axis=0, tiled=False)

    pw_own = pl.pallas_call(
        places_kernel, out_shape=like((32, 2 * rows), F32), in_specs=[VMEM, VMEM], out_specs=VMEM, name="places"
    )(expert_ids, route_weights)
    pw = lax.all_to_all(pw_own, ZY, split_axis=0, concat_axis=0, tiled=True)

    strip = (2, f, 512)
    outgoing = pl.pallas_call(
        outgoing_kernel,
        grid_spec=prefetched(
            (4,),
            [pl.BlockSpec(strip, lambda j, cr: (0, 0, 2 * j + 1 - cr[0]))] * 3,
            pl.BlockSpec((6, f, 512), lambda j, cr: (0, 0, j)),
        ),
        out_shape=like((6, f, half)),
        cost_estimate=cost(0, 9.4e6),
        name="outgoing",
    )(cs, w_gate, w_up, w_down)
    incoming = swap(outgoing)
    wgu, wd = pl.pallas_call(
        assemble_kernel,
        grid_spec=prefetched(
            (4,),
            [pl.BlockSpec(strip, lambda j, cr: (0, 0, 2 * j + cr[0]))] * 3
            + [pl.BlockSpec((6, f, 512), lambda j, cr: (0, 0, j))],
            [
                pl.BlockSpec((2, 4 * f, 512), lambda j, cr: (0, 0, j)),
                pl.BlockSpec((2, 2 * f, 512), lambda j, cr: (0, 0, j)),
            ],
        ),
        out_shape=(like((2, 4 * f, half)), like((2, 2 * f, half))),
        compiler_params=params(32),
        cost_estimate=cost(0, 19e6),
        name="assemble",
    )(cs, w_gate, w_up, w_down, incoming)

    xs, gs = pl.pallas_call(
        select_kernel,
        grid=(8,),
        out_shape=(like((2, slots, half)), like((2, slots, half))),
        in_specs=[VMEM, pl.BlockSpec((8, rows, 1024), lambda b: (b, 0, 0))],
        out_specs=(
            pl.BlockSpec((2, 2 * CAP, half), lambda b: (0, b, 0)),
            pl.BlockSpec((2, 2 * CAP, half), lambda b: (0, b, 0)),
        ),
        compiler_params=params(32),
        cost_estimate=cost(3.2e9, 30e6),
        name="select",
    )(pw, gathered)

    def hidden(which):
        return pl.pallas_call(
            hidden_kernel,
            grid_spec=prefetched(
                (4,),
                [
                    pl.BlockSpec((1, slots, 512), lambda j, er: (er[0], 0, j)),
                    pl.BlockSpec((1, slots, 512), lambda j, er: (er[0], 0, j)),
                    pl.BlockSpec((1, 4 * f, 512), lambda j, er: (er[0], 0, j)),
                    pl.BlockSpec((1, 2 * f, 512), lambda j, er: (er[0], 0, j)),
                ],
                pl.BlockSpec((slots, 6 * f), lambda j, er: (0, 0)),
            ),
            out_shape=like((slots, 6 * f), F32),
            compiler_params=params(40),
            cost_estimate=cost(2 * slots * half * 6 * f, 15e6),
            name="hidden",
        )(which, xs, gs, wgu, wd)

    received = swap(hidden(others))
    mine = pl.pallas_call(
        act_kernel,
        grid=(4,),
        out_shape=like((slots, 6 * f)),
        in_specs=[pl.BlockSpec((slots // 4, 6 * f), lambda j: (j, 0))] * 2,
        out_specs=pl.BlockSpec((slots // 4, 6 * f), lambda j: (j, 0)),
        compiler_params=params(32),
        cost_estimate=cost(1e7, 9e6),
        name="act",
    )(hidden(cs), received)
    theirs = swap(mine)

    def partial(which, place, ad, into):
        specs = [VMEM, pl.BlockSpec((1, 4 * f, 512), lambda j, er: (er[0], 0, j))]
        out = like((16, 4, 2, CAP, 512))
        return pl.pallas_call(
            partial_kernel,
            grid_spec=prefetched(
                (4,),
                specs + [pl.BlockSpec(memory_space=pl.ANY)] * len(into),
                pl.BlockSpec((16, 1, 1, CAP, 512), lambda j, er: (0, j, place, 0, 0)),
            ),
            out_shape=out,
            input_output_aliases={3: 0} if into else {},
            compiler_params=params(32),
            cost_estimate=cost(2 * slots * half * 4 * f, 8e6),
            name="partial",
        )(which, ad, wgu, *into)

    sent = partial(others, 1, theirs, [partial(cs, 0, mine, [])])
    returned = lax.all_to_all(sent.reshape(64, 2, CAP, 512), ZYX, split_axis=0, concat_axis=0, tiled=True)

    pick = lambda i, cr: jnp.where(i == 0, cr[0], 1 - cr[0])
    gg, gu, gd, send = pl.pallas_call(
        weight_kernel,
        grid_spec=prefetched(
            (2, 4),
            [
                VMEM,
                VMEM,
                pl.BlockSpec((1, slots, 512), lambda i, j, cr: (pick(i, cr), 0, j)),
                pl.BlockSpec((1, slots, 512), lambda i, j, cr: (pick(i, cr), 0, j)),
            ],
            [pl.BlockSpec((1, f, 512), lambda i, j, cr: (pick(i, cr), 0, 2 * j + cr[0]))] * 3
            + [pl.BlockSpec((1, 3, f, 512), lambda i, j, cr: (pick(i, cr), 0, 0, j))],
            [pltpu.VMEM((6 * f, slots), BF)],
        ),
        out_shape=[like((2, f, width))] * 3 + [like((2, 3, f, half))],
        compiler_params=params(40),
        cost_estimate=cost(4 * slots * half * 6 * f, 24e6),
        name="weights",
    )(cs, mine, theirs, xs, gs)
    strips = pl.BlockSpec(strip, lambda j, cr: (0, 0, 2 * j + 1 - cr[0]))
    grads = pl.pallas_call(
        settle_kernel,
        grid_spec=prefetched(
            (4,),
            [pl.BlockSpec((2, 3, f, 512), lambda j, cr: (0, 0, 0, j))] + [pl.BlockSpec(memory_space=pl.ANY)] * 3,
            [strips] * 3,
        ),
        out_shape=[like((2, f, width))] * 3,
        input_output_aliases={2: 0, 3: 1, 4: 2},
        cost_estimate=cost(0, 9.4e6),
        name="settle",
    )(cs, swap(send), gg, gu, gd)

    grad_tokens = pl.pallas_call(
        combine_kernel,
        out_shape=like((rows, 512)),
        in_specs=[SMEM, VMEM, VMEM],
        out_specs=VMEM,
        compiler_params=params(40),
        cost_estimate=cost(1e9, 6.5e6),
        name="combine",
    )(cs, pw_own, returned.reshape(16, 4, 2 * CAP, 512))
    return (grad_tokens, *grads)


def solution(mesh):
    fine = Mesh(mesh.devices.reshape(4, 4, 4, 2), ("z", "y", "x", "c"))
    rows = P(ZY, None)
    weights = P(ZY, ("x", "c"), None)
    return jax.shard_map(
        shards,
        mesh=fine,
        in_specs=(rows, rows, rows, rows, weights, weights, weights),
        out_specs=(P(ZY, ("x", "c")), weights, weights, weights),
        check_vma=False,
    )
```

```python
import jax
import jax.numpy as jnp
from jax import lax
from jax.experimental import pallas as pl
from jax.experimental.pallas import tpu as pltpu
from jax.sharding import Mesh
from jax.sharding import PartitionSpec as P

BF = jnp.bfloat16
F32 = jnp.float32
CAP = 48
ZY = ("z", "y")
ZYX = ("z", "y", "x")
VMEM = pl.BlockSpec(memory_space=pltpu.VMEM)
SMEM = pl.BlockSpec(memory_space=pltpu.SMEM)
SWAP = [(0, 1), (1, 0)]


def params(mib):
    return pltpu.CompilerParams(vmem_limit_bytes=mib * 1024 * 1024)


def cost(flops, nbytes):
    return pl.CostEstimate(flops=int(flops / 1e3), bytes_accessed=int(nbytes / 1e3), transcendentals=0)


def nt(a, b):
    return lax.dot_general(a, b, (((1,), (1,)), ((), ())), preferred_element_type=F32)


def mm(a, b):
    return jnp.dot(a, b, preferred_element_type=F32)


def swap(v):
    return lax.ppermute(v, "c", SWAP)


def pairs(to):
    spot = lambda z, y, x, c: ((z % 4 * 4 + y % 4) * 4 + x % 4) * 2 + c
    places = [(z, y, x, c) for z in range(4) for y in range(4) for x in range(4) for c in range(2)]
    return [(spot(*p), spot(*to(*p))) for p in places]


def first(s):
    return pairs(lambda z, y, x, c: (z + s, y, x, c) if c == 0 else (z, y + s, x, c))


def second(s):
    return pairs(lambda z, y, x, c: (z, y + s, x, c) if c == 0 else (z + s, y, x, c))


along = pairs(lambda z, y, x, c: (z, y, x + 1 if c == 0 else x - 1, c))


def hop(v, to):
    return lax.ppermute(v, ("z", "y", "x", "c"), to)


def together(*v):
    return lax.optimization_barrier(v)


def like(shape, dtype=BF):
    return jax.ShapeDtypeStruct(shape, dtype)


def prefetched(grid, in_specs, out_specs, scratch=()):
    return pltpu.PrefetchScalarGridSpec(
        num_scalar_prefetch=1, grid=grid, in_specs=in_specs, out_specs=out_specs, scratch_shapes=list(scratch)
    )


def pack_kernel(at_ref, ids_ref, wts_ref, t0, t1, g0, g1, g2, g3, out_ref):
    top, rows = ids_ref.shape
    expert = lax.broadcasted_iota(jnp.int32, (32, rows), 0)
    hit = jnp.zeros((32, rows), F32)
    wt = jnp.zeros((32, rows), F32)
    for k in range(top):
        same = ids_ref[k : k + 1, :] == expert
        hit = hit + same.astype(F32)
        wt = wt + jnp.where(same, wts_ref[k : k + 1, :], 0.0)
    r = lax.broadcasted_iota(jnp.int32, (rows, rows), 0)
    q = lax.broadcasted_iota(jnp.int32, (rows, rows), 1)
    before = mm(hit.astype(BF), (r < q).astype(BF))
    pos = jnp.where(hit > 0.5, before, -1.0)
    high = wt.astype(BF)
    rest = wt - high.astype(F32)
    mid = rest.astype(BF)
    low = (rest - mid.astype(F32)).astype(BF)
    out_ref[:, 0:512] = t0[...]
    out_ref[:, 512:1024] = t1[...]
    out_ref[:, 1024:1152] = jnp.concatenate([pos.astype(BF), high, mid, low], axis=0)
    for i, ref in enumerate((g0, g1, g2, g3)):
        out_ref[:, 1152 + i * 512 : 1664 + i * 512] = ref[...]


def chosen(row):
    p = lax.broadcasted_iota(jnp.int32, (CAP, row.shape[1]), 0).astype(F32)
    return row == p


def outgoing_kernel(c_ref, g_ref, u_ref, d_ref, out_ref):
    out_ref[0:2] = g_ref[...]
    out_ref[2:4] = u_ref[...]
    out_ref[4:6] = d_ref[...]


def assemble_kernel(c_ref, g_ref, u_ref, d_ref, in_ref, wgu_ref, wd_ref):
    f = g_ref.shape[1]

    def place(low, high):
        for e in range(2):
            wgu_ref[e, low : low + f] = g_ref[e]
            wgu_ref[e, high : high + f] = in_ref[e]
            wgu_ref[e, 2 * f + low : 3 * f + low] = u_ref[e]
            wgu_ref[e, 2 * f + high : 3 * f + high] = in_ref[2 + e]
            wd_ref[e, low : low + f] = d_ref[e]
            wd_ref[e, high : high + f] = in_ref[4 + e]

    @pl.when(c_ref[0] == 0)
    def _():
        place(0, f)

    @pl.when(c_ref[0] == 1)
    def _():
        place(f, 0)


def picked(info_ref, meta, held):
    held[...] = meta.astype(F32)
    picks, scales = [], []
    for k in range(2):
        row = info_ref[0] + k
        pick = chosen(held[pl.ds(row, 1), :])
        wt = held[pl.ds(32 + row, 1), :] + held[pl.ds(64 + row, 1), :] + held[pl.ds(96 + row, 1), :]
        picks.append(pick.astype(F32))
        scales.append(jnp.sum(jnp.where(pick, wt, 0.0), axis=1, keepdims=True))
    return jnp.concatenate(picks, axis=0).astype(BF), jnp.concatenate(scales, axis=0)


def select_x_kernel(info_ref, near_ref, far_ref, *rest):
    out_ref, held = rest[-2:]
    w = out_ref.shape[2] // 2
    pick, _ = picked(info_ref, near_ref[0, :, w:], held)
    for i, ref in enumerate((near_ref, far_ref)):
        got = mm(pick, ref[0, :, 0:w]).astype(BF)
        side = info_ref[1] if i == 0 else 1 - info_ref[1]
        cols = pl.ds(pl.multiple_of(side * w, w), w)
        out_ref[0, :, cols] = got[0:CAP]
        out_ref[1, :, cols] = got[CAP:]


def select_g_kernel(info_ref, near_ref, g_ref, *rest):
    out_ref, held = rest[-2:]
    pick, scale = picked(info_ref, near_ref[0], held)
    got = (mm(pick, g_ref[0]) * scale).astype(BF)
    out_ref[0] = got[0:CAP]
    out_ref[1] = got[CAP:]


def hidden_kernel(e_ref, v_ref, w_ref, out_ref):
    out_ref[...] = nt(v_ref[0], w_ref[0])


def act_kernel(a_ref, b_ref, d_ref, e_ref, out_ref):
    n = out_ref.shape[1] // 3
    h = a_ref[...] + b_ref[...]
    gate, up = h[:, 0:n], h[:, n:]
    d = d_ref[...] + e_ref[...]
    sig = jax.nn.sigmoid(gate)
    silu = gate * sig
    out_ref[:, 0:n] = (d * up * sig * (1.0 + gate * (1.0 - sig))).astype(BF)
    out_ref[:, n : 2 * n] = (d * silu).astype(BF)
    out_ref[:, 2 * n :] = (silu * up).astype(BF)


def partial_kernel(e_ref, ad_ref, wgu_ref, *rest):
    out_ref = rest[-1]
    n = wgu_ref.shape[1]
    got = mm(ad_ref[:, 0:n], wgu_ref[0]).astype(BF)
    out_ref[:, 0, 0] = got.reshape(16, CAP, 512)


def weight_kernel(c_ref, mine_ref, theirs_ref, xs_ref, gs_ref, gg_ref, gu_ref, gd_ref, send_ref, dt):
    f = gg_ref.shape[1]
    first = pl.program_id(1) == 0

    @pl.when(first & (pl.program_id(0) == 0))
    def _():
        dt[...] = mine_ref[...].astype(F32).T.astype(BF)

    @pl.when(first & (pl.program_id(0) == 1))
    def _():
        dt[...] = theirs_ref[...].astype(F32).T.astype(BF)

    c = c_ref[0]
    outs = (gg_ref, gu_ref, gd_ref)
    for i in range(3):
        rows = xs_ref if i < 2 else gs_ref
        keep = pl.ds(pl.multiple_of(2 * f * i + f * c, f), f)
        away = pl.ds(pl.multiple_of(2 * f * i + f * (1 - c), f), f)
        outs[i][0] = mm(dt[keep, :], rows[0]).astype(BF)
        send_ref[0, i] = mm(dt[away, :], rows[0]).astype(BF)


def settle_kernel(c_ref, in_ref, a_ref, b_ref, d_ref, gg_ref, gu_ref, gd_ref):
    for e in range(2):
        gg_ref[e] = in_ref[e, 0]
        gu_ref[e] = in_ref[e, 1]
        gd_ref[e] = in_ref[e, 2]


def combine_kernel(c_ref, pw_ref, ret_ref, out_ref):
    low = c_ref[0] == 0
    places = pw_ref[0:32, 1024:1152].astype(F32)
    picks = []
    for e in range(16):
        a, b = places[2 * e : 2 * e + 1], places[2 * e + 1 : 2 * e + 2]
        picks.append(chosen(jnp.where(low, a, b)).astype(F32))
        picks.append(chosen(jnp.where(low, b, a)).astype(F32))
    pick = jnp.concatenate(picks, axis=0).T.astype(BF)
    total = mm(pick, ret_ref[:, 0].reshape(32 * CAP, 512))
    for x in range(1, 4):
        total = total + mm(pick, ret_ref[:, x].reshape(32 * CAP, 512))
    out_ref[...] = total.astype(BF)


def shards(tokens, expert_ids, route_weights, grad_out, w_gate, w_up, w_down):
    rows, width = tokens.shape
    f = w_gate.shape[1]
    slots = 16 * CAP
    half = width // 2
    c = lax.axis_index("c")
    x = lax.axis_index("x")
    cs = jnp.reshape(c, (1,)).astype(jnp.int32)
    others = 1 - cs

    z, y = lax.axis_index("z"), lax.axis_index("y")
    side = x % 2

    piece = lambda k: pl.BlockSpec((rows, 512), lambda i, ar: (0, ar[k]))
    flat = lambda v: pl.BlockSpec(v.shape, lambda i, ar: (0, 0))
    ids, wts = expert_ids.T, route_weights.T
    own = pl.pallas_call(
        pack_kernel,
        grid_spec=prefetched(
            (1,),
            [flat(ids), flat(wts)] + [piece(k) for k in range(6)],
            pl.BlockSpec((rows, 3200), lambda i, ar: (0, 0)),
        ),
        out_shape=like((rows, 3200)),
        cost_estimate=cost(1e7, 2e6),
        name="pack",
    )(
        jnp.stack([2 * k + c for k in (2 * side, 2 * side + 1, 0, 1, 2, 3)]).astype(jnp.int32),
        *(ids, wts, tokens, tokens, grad_out, grad_out, grad_out, grad_out),
    )

    strip = (2, f, 512)
    outgoing = pl.pallas_call(
        outgoing_kernel,
        grid_spec=prefetched(
            (4,),
            [pl.BlockSpec(strip, lambda j, cr: (0, 0, 2 * j + 1 - cr[0]))] * 3,
            pl.BlockSpec((6, f, 512), lambda j, cr: (0, 0, j)),
        ),
        out_shape=like((6, f, half)),
        cost_estimate=cost(0, 9.4e6),
        name="outgoing",
    )(cs, w_gate, w_up, w_down)

    up, down = hop(own, first(1)), hop(own, first(-1))
    up, down, outgoing = together(up, down, outgoing)
    far = jnp.concatenate([hop(up[:64], first(1)), hop(down[64:], first(-1))], axis=0)
    incoming = swap(outgoing)
    line = [own, up, down, far]
    xg = jnp.stack([v[:, :1152] for v in line])
    gg = jnp.stack([v[:, 1152:] for v in line])
    xm, xr, xg_far = hop(xg, second(1)), hop(xg, second(-1)), hop(xg, along)
    gg, xm, xr, xg_far, incoming = together(gg, xm, xr, xg_far, incoming)
    gm, gr = hop(gg, second(1)), hop(gg, second(-1))
    xd0, xd1 = hop(xm[:2], second(1)), hop(xr[2:], second(-1))
    xm_far = hop(xm, along)

    wgu, wd = pl.pallas_call(
        assemble_kernel,
        grid_spec=prefetched(
            (4,),
            [pl.BlockSpec(strip, lambda j, cr: (0, 0, 2 * j + cr[0]))] * 3
            + [pl.BlockSpec((6, f, 512), lambda j, cr: (0, 0, j))],
            [
                pl.BlockSpec((2, 4 * f, 512), lambda j, cr: (0, 0, j)),
                pl.BlockSpec((2, 2 * f, 512), lambda j, cr: (0, 0, j)),
            ],
        ),
        out_shape=(like((2, 4 * f, half)), like((2, 2 * f, half))),
        compiler_params=params(24),
        cost_estimate=cost(0, 19e6),
        name="assemble",
    )(cs, w_gate, w_up, w_down, incoming)

    offsets = (0, -1, 1, 2)
    table = []
    for b in offsets:
        for a in offsets:
            oz, oy = jnp.where(c == 0, a, b), jnp.where(c == 0, b, a)
            table.append((z + oz + 4) % 4 * 4 + (y + oy + 4) % 4)
    info = jnp.stack([2 * (z * 4 + y), side] + table).astype(jnp.int32)

    def select(kernel, start, near, other, into):
        is_x = kernel is select_x_kernel
        if is_x:
            specs = [pl.BlockSpec((1, rows, 1152), lambda i, fo: (i, 0, 0))] * 2
        else:
            specs = [
                pl.BlockSpec((1, rows, 128), lambda i, fo: (i, 0, 8)),
                pl.BlockSpec((1, rows, half), lambda i, fo: (i, 0, 0)),
            ]
        n = near.shape[0]
        return pl.pallas_call(
            kernel,
            grid_spec=prefetched(
                (n,),
                specs + [pl.BlockSpec(memory_space=pl.ANY)] * len(into),
                pl.BlockSpec((2, CAP, half), lambda i, fo: (0, fo[2 + start + i], 0)),
                [pltpu.VMEM((rows, rows), F32)],
            ),
            out_shape=like((2, slots, half)),
            input_output_aliases={3: 0} if into else {},
            compiler_params=params(24),
            cost_estimate=cost(2 * n * 2 * CAP * rows * half, n * 1.4e6),
            name="select",
        )(info, near, other, *into)

    xs = select(select_x_kernel, 0, xg, xg_far, [])
    gs = select(select_g_kernel, 0, xg, gg, [])
    xm_far, xr_go, xs, gs, wgu, wd = together(xm_far, xr, xs, gs, wgu, wd)
    xr_far = hop(xr_go, along)
    gm, gr, xd0, xd1, xr_far = together(gm, gr, xd0, xd1, xr_far)
    gd0, gd1 = hop(gm[:2], second(1)), hop(gr[2:], second(-1))
    xd0_far = hop(xd0, along)
    xs = select(select_x_kernel, 4, xm, xm_far, [xs])
    gs = select(select_g_kernel, 4, xm, gm, [gs])
    xd0_far, xd1, xs, gs = together(xd0_far, xd1, xs, gs)
    xd1_far = hop(xd1, along)
    xs = select(select_x_kernel, 8, xr, xr_far, [xs])
    xs = select(select_x_kernel, 12, xd0, xd0_far, [xs])
    gs = select(select_g_kernel, 8, xr, gr, [gs])
    xs = select(select_x_kernel, 14, xd1, xd1_far, [xs])
    gd0, gd1, xs, gs = together(gd0, gd1, xs, gs)
    gs = select(select_g_kernel, 12, xd0, gd0, [gs])
    gs = select(select_g_kernel, 14, xd1, gd1, [gs])

    def hidden(which, v, w, chunk):
        n = w.shape[1]
        return pl.pallas_call(
            hidden_kernel,
            grid_spec=prefetched(
                (n // chunk,),
                [
                    pl.BlockSpec((1, slots, half), lambda j, er: (er[0], 0, 0)),
                    pl.BlockSpec((1, chunk, half), lambda j, er: (er[0], j, 0)),
                ],
                pl.BlockSpec((slots, chunk), lambda j, er: (0, j)),
            ),
            out_shape=like((slots, n), F32),
            compiler_params=params(24),
            cost_estimate=cost(2 * slots * half * n, 9e6),
            name="hidden",
        )(which, v, w)

    pre_in = swap(hidden(others, xs, wgu, 256))
    pre = hidden(cs, xs, wgu, 256)
    dh_in = swap(hidden(others, gs, wd, 128))
    dh = hidden(cs, gs, wd, 128)
    quarter = lambda n: pl.BlockSpec((slots // 4, n), lambda j: (j, 0))
    mine = pl.pallas_call(
        act_kernel,
        grid=(4,),
        out_shape=like((slots, 6 * f)),
        in_specs=[quarter(4 * f), quarter(4 * f), quarter(2 * f), quarter(2 * f)],
        out_specs=quarter(6 * f),
        compiler_params=params(24),
        cost_estimate=cost(1e7, 9e6),
        name="act",
    )(pre, pre_in, dh, dh_in)
    theirs = swap(mine)

    def partial(which, place, ad, into):
        specs = [VMEM, pl.BlockSpec((1, 4 * f, 512), lambda j, er: (er[0], 0, j))]
        out = like((16, 4, 2, CAP, 512))
        return pl.pallas_call(
            partial_kernel,
            grid_spec=prefetched(
                (4,),
                specs + [pl.BlockSpec(memory_space=pl.ANY)] * len(into),
                pl.BlockSpec((16, 1, 1, CAP, 512), lambda j, er: (0, j, place, 0, 0)),
            ),
            out_shape=out,
            input_output_aliases={3: 0} if into else {},
            compiler_params=params(24),
            cost_estimate=cost(2 * slots * half * 4 * f, 8e6),
            name="partial",
        )(which, ad, wgu, *into)

    sent = partial(others, 1, theirs, [partial(cs, 0, mine, [])])
    returned = lax.all_to_all(sent.reshape(64, 2, CAP, 512), ZYX, split_axis=0, concat_axis=0, tiled=True)

    pick = lambda i, cr: jnp.where(i == 0, cr[0], 1 - cr[0])
    gg, gu, gd, send = pl.pallas_call(
        weight_kernel,
        grid_spec=prefetched(
            (2, 4),
            [
                VMEM,
                VMEM,
                pl.BlockSpec((1, slots, 512), lambda i, j, cr: (pick(i, cr), 0, j)),
                pl.BlockSpec((1, slots, 512), lambda i, j, cr: (pick(i, cr), 0, j)),
            ],
            [pl.BlockSpec((1, f, 512), lambda i, j, cr: (pick(i, cr), 0, 2 * j + cr[0]))] * 3
            + [pl.BlockSpec((1, 3, f, 512), lambda i, j, cr: (pick(i, cr), 0, 0, j))],
            [pltpu.VMEM((6 * f, slots), BF)],
        ),
        out_shape=[like((2, f, width))] * 3 + [like((2, 3, f, half))],
        compiler_params=params(24),
        cost_estimate=cost(4 * slots * half * 6 * f, 24e6),
        name="weights",
    )(cs, mine, theirs, xs, gs)
    strips = pl.BlockSpec(strip, lambda j, cr: (0, 0, 2 * j + 1 - cr[0]))
    grads = pl.pallas_call(
        settle_kernel,
        grid_spec=prefetched(
            (4,),
            [pl.BlockSpec((2, 3, f, 512), lambda j, cr: (0, 0, 0, j))] + [pl.BlockSpec(memory_space=pl.ANY)] * 3,
            [strips] * 3,
        ),
        out_shape=[like((2, f, width))] * 3,
        input_output_aliases={2: 0, 3: 1, 4: 2},
        cost_estimate=cost(0, 9.4e6),
        name="settle",
    )(cs, swap(send), gg, gu, gd)

    grad_tokens = pl.pallas_call(
        combine_kernel,
        out_shape=like((rows, 512)),
        in_specs=[SMEM, VMEM, VMEM],
        out_specs=VMEM,
        compiler_params=params(24),
        cost_estimate=cost(1e9, 6.5e6),
        name="combine",
    )(cs, own, returned.reshape(16, 4, 2 * CAP, 512))
    return (grad_tokens, *grads)


def solution(mesh):
    fine = Mesh(mesh.devices.reshape(4, 4, 4, 2), ("z", "y", "x", "c"))
    rows = P(ZY, None)
    weights = P(ZY, ("x", "c"), None)
    return jax.shard_map(
        shards,
        mesh=fine,
        in_specs=(rows, rows, rows, rows, weights, weights, weights),
        out_specs=(P(ZY, ("x", "c")), weights, weights, weights),
        check_vma=False,
    )
```

```python
import jax
import jax.numpy as jnp
from jax import lax
from jax.experimental import pallas as pl
from jax.experimental.pallas import tpu as pltpu
from jax.sharding import Mesh
from jax.sharding import PartitionSpec as P

BF = jnp.bfloat16
F32 = jnp.float32
CAP = 48
ZY = ("z", "y")
ZYX = ("z", "y", "x")
VMEM = pl.BlockSpec(memory_space=pltpu.VMEM)
SMEM = pl.BlockSpec(memory_space=pltpu.SMEM)
SWAP = [(0, 1), (1, 0)]


def params(mib):
    return pltpu.CompilerParams(vmem_limit_bytes=mib * 1024 * 1024)


def cost(flops, nbytes):
    return pl.CostEstimate(flops=int(flops / 1e3), bytes_accessed=int(nbytes / 1e3), transcendentals=0)


def nt(a, b):
    return lax.dot_general(a, b, (((1,), (1,)), ((), ())), preferred_element_type=F32)


def mm(a, b):
    return jnp.dot(a, b, preferred_element_type=F32)


def swap(v):
    return lax.ppermute(v, "c", SWAP)


def pairs(to):
    spot = lambda z, y, x, c: ((z % 4 * 4 + y % 4) * 4 + x % 4) * 2 + c
    places = [(z, y, x, c) for z in range(4) for y in range(4) for x in range(4) for c in range(2)]
    return [(spot(*p), spot(*to(*p))) for p in places]


def first(s):
    return pairs(lambda z, y, x, c: (z + s, y, x, c) if c == 0 else (z, y + s, x, c))


def second(s):
    return pairs(lambda z, y, x, c: (z, y + s, x, c) if c == 0 else (z + s, y, x, c))


along = pairs(lambda z, y, x, c: (z, y, x + 1 if c == 0 else x - 1, c))


def hop(v, to):
    return lax.ppermute(v, ("z", "y", "x", "c"), to)


def together(*v):
    return lax.optimization_barrier(v)


def like(shape, dtype=BF):
    return jax.ShapeDtypeStruct(shape, dtype)


def prefetched(grid, in_specs, out_specs, scratch=()):
    return pltpu.PrefetchScalarGridSpec(
        num_scalar_prefetch=1, grid=grid, in_specs=in_specs, out_specs=out_specs, scratch_shapes=list(scratch)
    )


def pack_kernel(at_ref, ids_ref, wts_ref, t0, t1, g0, g1, g2, g3, out_ref):
    top, rows = ids_ref.shape
    expert = lax.broadcasted_iota(jnp.int32, (32, rows), 0)
    hit = jnp.zeros((32, rows), F32)
    wt = jnp.zeros((32, rows), F32)
    for k in range(top):
        same = ids_ref[k : k + 1, :] == expert
        hit = hit + same.astype(F32)
        wt = wt + jnp.where(same, wts_ref[k : k + 1, :], 0.0)
    r = lax.broadcasted_iota(jnp.int32, (rows, rows), 0)
    q = lax.broadcasted_iota(jnp.int32, (rows, rows), 1)
    before = mm(hit.astype(BF), (r < q).astype(BF))
    pos = jnp.where(hit > 0.5, before, -1.0)
    high = wt.astype(BF)
    rest = wt - high.astype(F32)
    mid = rest.astype(BF)
    low = (rest - mid.astype(F32)).astype(BF)
    out_ref[:, 0:512] = t0[...]
    out_ref[:, 512:1024] = t1[...]
    out_ref[:, 1024:1152] = jnp.concatenate([pos.astype(BF), high, mid, low], axis=0)
    for i, ref in enumerate((g0, g1, g2, g3)):
        out_ref[:, 1152 + i * 512 : 1664 + i * 512] = ref[...]


def chosen(row):
    p = lax.broadcasted_iota(jnp.int32, (CAP, row.shape[1]), 0).astype(F32)
    return row == p


def outgoing_kernel(c_ref, g_ref, u_ref, d_ref, out_ref):
    out_ref[0:2] = g_ref[...]
    out_ref[2:4] = u_ref[...]
    out_ref[4:6] = d_ref[...]


def assemble_kernel(c_ref, g_ref, u_ref, d_ref, in_ref, wgu_ref, wd_ref):
    f = g_ref.shape[1]

    def place(low, high):
        for e in range(2):
            wgu_ref[e, low : low + f] = g_ref[e]
            wgu_ref[e, high : high + f] = in_ref[e]
            wgu_ref[e, 2 * f + low : 3 * f + low] = u_ref[e]
            wgu_ref[e, 2 * f + high : 3 * f + high] = in_ref[2 + e]
            wd_ref[e, low : low + f] = d_ref[e]
            wd_ref[e, high : high + f] = in_ref[4 + e]

    @pl.when(c_ref[0] == 0)
    def _():
        place(0, f)

    @pl.when(c_ref[0] == 1)
    def _():
        place(f, 0)


def picked(info_ref, meta, held):
    held[...] = meta.astype(F32)
    picks, scales = [], []
    for k in range(2):
        row = info_ref[0] + k
        pick = chosen(held[pl.ds(row, 1), :])
        wt = held[pl.ds(32 + row, 1), :] + held[pl.ds(64 + row, 1), :] + held[pl.ds(96 + row, 1), :]
        picks.append(pick.astype(F32))
        scales.append(jnp.sum(jnp.where(pick, wt, 0.0), axis=1, keepdims=True))
    return jnp.concatenate(picks, axis=0).astype(BF), jnp.concatenate(scales, axis=0)


def select_x_kernel(info_ref, near_ref, far_ref, *rest):
    out_ref, held = rest[-2:]
    w = out_ref.shape[2] // 2
    pick, _ = picked(info_ref, near_ref[0, :, w:], held)
    for i, ref in enumerate((near_ref, far_ref)):
        got = mm(pick, ref[0, :, 0:w]).astype(BF)
        side = info_ref[1] if i == 0 else 1 - info_ref[1]
        cols = pl.ds(pl.multiple_of(side * w, w), w)
        out_ref[0, :, cols] = got[0:CAP]
        out_ref[1, :, cols] = got[CAP:]


def select_g_kernel(info_ref, near_ref, g_ref, *rest):
    out_ref, held = rest[-2:]
    pick, scale = picked(info_ref, near_ref[0], held)
    got = (mm(pick, g_ref[0]) * scale).astype(BF)
    out_ref[0] = got[0:CAP]
    out_ref[1] = got[CAP:]


def hidden_kernel(e_ref, v_ref, w_ref, out_ref):
    out_ref[...] = nt(v_ref[0], w_ref[0])


def act_kernel(a_ref, b_ref, d_ref, e_ref, out_ref):
    n = out_ref.shape[1] // 3
    h = a_ref[...] + b_ref[...]
    gate, up = h[:, 0:n], h[:, n:]
    d = d_ref[...] + e_ref[...]
    sig = jax.nn.sigmoid(gate)
    silu = gate * sig
    out_ref[:, 0:n] = (d * up * sig * (1.0 + gate * (1.0 - sig))).astype(BF)
    out_ref[:, n : 2 * n] = (d * silu).astype(BF)
    out_ref[:, 2 * n :] = (silu * up).astype(BF)


def partial_kernel(e_ref, ad_ref, wgu_ref, *rest):
    ring_ref, rows_ref = rest[-2:]
    n = wgu_ref.shape[1]
    got = mm(ad_ref[:, 0:n], wgu_ref[0]).astype(BF)
    ring_ref[0, 0] = got[:, 0:256]
    rows_ref[:, 0] = got[:, 256:512].reshape(16, CAP, 256)


def weight_kernel(c_ref, mine_ref, theirs_ref, xs_ref, gs_ref, gg_ref, gu_ref, gd_ref, send_ref, dt):
    f = gg_ref.shape[1]
    first = pl.program_id(1) == 0

    @pl.when(first & (pl.program_id(0) == 0))
    def _():
        dt[...] = mine_ref[...].astype(F32).T.astype(BF)

    @pl.when(first & (pl.program_id(0) == 1))
    def _():
        dt[...] = theirs_ref[...].astype(F32).T.astype(BF)

    c = c_ref[0]
    outs = (gg_ref, gu_ref, gd_ref)
    for i in range(3):
        rows = xs_ref if i < 2 else gs_ref
        keep = pl.ds(pl.multiple_of(2 * f * i + f * c, f), f)
        away = pl.ds(pl.multiple_of(2 * f * i + f * (1 - c), f), f)
        outs[i][0] = mm(dt[keep, :], rows[0]).astype(BF)
        send_ref[0, i] = mm(dt[away, :], rows[0]).astype(BF)


def settle_kernel(c_ref, in_ref, a_ref, b_ref, d_ref, gg_ref, gu_ref, gd_ref):
    for e in range(2):
        gg_ref[e] = in_ref[e, 0]
        gu_ref[e] = in_ref[e, 1]
        gd_ref[e] = in_ref[e, 2]


def gathering(c_ref, pw_ref):
    low = c_ref[0] == 0
    places = pw_ref[0:32, 1024:1152].astype(F32)
    picks = []
    for e in range(16):
        a, b = places[2 * e : 2 * e + 1], places[2 * e + 1 : 2 * e + 2]
        picks.append(chosen(jnp.where(low, a, b)).astype(F32))
        picks.append(chosen(jnp.where(low, b, a)).astype(F32))
    return jnp.concatenate(picks, axis=0).T.astype(BF)


def rows_kernel(c_ref, pw_ref, ret_ref, out_ref):
    total = mm(gathering(c_ref, pw_ref), ret_ref[...].reshape(32 * CAP, 1024))
    for j in range(4):
        out_ref[lax.rem(j - c_ref[1] + 4, 4)] = total[:, j * 256 : (j + 1) * 256]


def combine_kernel(c_ref, pw_ref, ret_ref, a_ref, b_ref, d_ref, e_ref, out_ref):
    out_ref[:, 0:256] = mm(gathering(c_ref, pw_ref), ret_ref[...].reshape(32 * CAP, 256)).astype(BF)
    out_ref[:, 256:512] = (a_ref[...] + b_ref[...] + d_ref[...] + e_ref[...]).astype(BF)


def shards(tokens, expert_ids, route_weights, grad_out, w_gate, w_up, w_down):
    rows, width = tokens.shape
    f = w_gate.shape[1]
    slots = 16 * CAP
    half = width // 2
    c = lax.axis_index("c")
    x = lax.axis_index("x")
    cs = jnp.reshape(c, (1,)).astype(jnp.int32)
    others = 1 - cs

    z, y = lax.axis_index("z"), lax.axis_index("y")
    side = x % 2

    piece = lambda k: pl.BlockSpec((rows, 512), lambda i, ar: (0, ar[k]))
    flat = lambda v: pl.BlockSpec(v.shape, lambda i, ar: (0, 0))
    ids, wts = expert_ids.T, route_weights.T
    own = pl.pallas_call(
        pack_kernel,
        grid_spec=prefetched(
            (1,),
            [flat(ids), flat(wts)] + [piece(k) for k in range(6)],
            pl.BlockSpec((rows, 3200), lambda i, ar: (0, 0)),
        ),
        out_shape=like((rows, 3200)),
        cost_estimate=cost(1e7, 2e6),
        name="pack",
    )(
        jnp.stack([2 * k + c for k in (2 * side, 2 * side + 1, 0, 1, 2, 3)]).astype(jnp.int32),
        *(ids, wts, tokens, tokens, grad_out, grad_out, grad_out, grad_out),
    )

    strip = (2, f, 512)
    outgoing = pl.pallas_call(
        outgoing_kernel,
        grid_spec=prefetched(
            (4,),
            [pl.BlockSpec(strip, lambda j, cr: (0, 0, 2 * j + 1 - cr[0]))] * 3,
            pl.BlockSpec((6, f, 512), lambda j, cr: (0, 0, j)),
        ),
        out_shape=like((6, f, half)),
        cost_estimate=cost(0, 9.4e6),
        name="outgoing",
    )(cs, w_gate, w_up, w_down)

    up, down = hop(own, first(1)), hop(own, first(-1))
    up, down, outgoing = together(up, down, outgoing)
    far = jnp.concatenate([hop(up[:64], first(1)), hop(down[64:], first(-1))], axis=0)
    incoming = swap(outgoing)
    line = [own, up, down, far]
    xg = jnp.stack([v[:, :1152] for v in line])
    gg = jnp.stack([v[:, 1152:] for v in line])
    xm, xr, xg_far = hop(xg, second(1)), hop(xg, second(-1)), hop(xg, along)
    gg, xm, xr, xg_far, incoming = together(gg, xm, xr, xg_far, incoming)
    gm, gr = hop(gg, second(1)), hop(gg, second(-1))
    xd0, xd1 = hop(xm[:2], second(1)), hop(xr[2:], second(-1))
    xm_far = hop(xm, along)

    wgu, wd = pl.pallas_call(
        assemble_kernel,
        grid_spec=prefetched(
            (4,),
            [pl.BlockSpec(strip, lambda j, cr: (0, 0, 2 * j + cr[0]))] * 3
            + [pl.BlockSpec((6, f, 512), lambda j, cr: (0, 0, j))],
            [
                pl.BlockSpec((2, 4 * f, 512), lambda j, cr: (0, 0, j)),
                pl.BlockSpec((2, 2 * f, 512), lambda j, cr: (0, 0, j)),
            ],
        ),
        out_shape=(like((2, 4 * f, half)), like((2, 2 * f, half))),
        compiler_params=params(24),
        cost_estimate=cost(0, 19e6),
        name="assemble",
    )(cs, w_gate, w_up, w_down, incoming)

    offsets = (0, -1, 1, 2)
    table = []
    for b in offsets:
        for a in offsets:
            oz, oy = jnp.where(c == 0, a, b), jnp.where(c == 0, b, a)
            table.append((z + oz + 4) % 4 * 4 + (y + oy + 4) % 4)
    info = jnp.stack([2 * (z * 4 + y), side] + table).astype(jnp.int32)

    def select(kernel, start, near, other, into):
        is_x = kernel is select_x_kernel
        if is_x:
            specs = [pl.BlockSpec((1, rows, 1152), lambda i, fo: (i, 0, 0))] * 2
        else:
            specs = [
                pl.BlockSpec((1, rows, 128), lambda i, fo: (i, 0, 8)),
                pl.BlockSpec((1, rows, half), lambda i, fo: (i, 0, 0)),
            ]
        n = near.shape[0]
        return pl.pallas_call(
            kernel,
            grid_spec=prefetched(
                (n,),
                specs + [pl.BlockSpec(memory_space=pl.ANY)] * len(into),
                pl.BlockSpec((2, CAP, half), lambda i, fo: (0, fo[2 + start + i], 0)),
                [pltpu.VMEM((rows, rows), F32)],
            ),
            out_shape=like((2, slots, half)),
            input_output_aliases={3: 0} if into else {},
            compiler_params=params(24),
            cost_estimate=cost(2 * n * 2 * CAP * rows * half, n * 1.4e6),
            name="select",
        )(info, near, other, *into)

    xs = select(select_x_kernel, 0, xg, xg_far, [])
    gs = select(select_g_kernel, 0, xg, gg, [])
    xm_far, xr_go, xs, gs, wgu, wd = together(xm_far, xr, xs, gs, wgu, wd)
    xr_far = hop(xr_go, along)
    gm, gr, xd0, xd1, xr_far = together(gm, gr, xd0, xd1, xr_far)
    gd0, gd1 = hop(gm[:2], second(1)), hop(gr[2:], second(-1))
    xd0_far = hop(xd0, along)
    xs = select(select_x_kernel, 4, xm, xm_far, [xs])
    gs = select(select_g_kernel, 4, xm, gm, [gs])
    xd0_far, xd1, xs, gs = together(xd0_far, xd1, xs, gs)
    xd1_far = hop(xd1, along)
    xs = select(select_x_kernel, 8, xr, xr_far, [xs])
    xs = select(select_x_kernel, 12, xd0, xd0_far, [xs])
    gs = select(select_g_kernel, 8, xr, gr, [gs])
    xs = select(select_x_kernel, 14, xd1, xd1_far, [xs])
    gd0, gd1, xs, gs = together(gd0, gd1, xs, gs)
    gs = select(select_g_kernel, 12, xd0, gd0, [gs])
    gs = select(select_g_kernel, 14, xd1, gd1, [gs])

    def hidden(which, v, w, chunk):
        n = w.shape[1]
        return pl.pallas_call(
            hidden_kernel,
            grid_spec=prefetched(
                (n // chunk,),
                [
                    pl.BlockSpec((1, slots, half), lambda j, er: (er[0], 0, 0)),
                    pl.BlockSpec((1, chunk, half), lambda j, er: (er[0], j, 0)),
                ],
                pl.BlockSpec((slots, chunk), lambda j, er: (0, j)),
            ),
            out_shape=like((slots, n), F32),
            compiler_params=params(24),
            cost_estimate=cost(2 * slots * half * n, 9e6),
            name="hidden",
        )(which, v, w)

    pre_in = swap(hidden(others, xs, wgu, 256))
    pre = hidden(cs, xs, wgu, 256)
    dh_in = swap(hidden(others, gs, wd, 128))
    dh = hidden(cs, gs, wd, 128)
    quarter = lambda n: pl.BlockSpec((slots // 4, n), lambda j: (j, 0))
    mine = pl.pallas_call(
        act_kernel,
        grid=(4,),
        out_shape=like((slots, 6 * f)),
        in_specs=[quarter(4 * f), quarter(4 * f), quarter(2 * f), quarter(2 * f)],
        out_specs=quarter(6 * f),
        compiler_params=params(24),
        cost_estimate=cost(1e7, 9e6),
        name="act",
    )(pre, pre_in, dh, dh_in)
    theirs = swap(mine)

    def partial(which, place, ad, into):
        specs = [VMEM, pl.BlockSpec((1, 4 * f, 512), lambda j, er: (er[0], 0, j))]
        return pl.pallas_call(
            partial_kernel,
            grid_spec=prefetched(
                (4,),
                specs + [pl.BlockSpec(memory_space=pl.ANY)] * len(into),
                [
                    pl.BlockSpec((1, 1, slots, 256), lambda j, er: (lax.rem(j - er[1] + 4, 4), place, 0, 0)),
                    pl.BlockSpec((16, 1, CAP, 256), lambda j, er: (0, place, 0, j)),
                ],
            ),
            out_shape=(like((4, 2, slots, 256)), like((16, 2, CAP, 1024))),
            input_output_aliases={3: 0, 4: 1} if into else {},
            compiler_params=params(24),
            cost_estimate=cost(2 * slots * half * 4 * f, 8e6),
            name="partial",
        )(jnp.concatenate([which, xx]), ad, wgu, *into)

    shift = lambda v, k: lax.ppermute(v, "x", [(i, (i + k) % 4) for i in range(4)])
    xx = jnp.reshape(x, (1,)).astype(jnp.int32)
    ring, by_rows = partial(others, 1, theirs, partial(cs, 0, mine, []))
    r1, r2, r3 = shift(ring[1], 1), shift(ring[2], 2), shift(ring[3], -1)
    by_rows, mine, theirs = together(by_rows, mine, theirs)
    row_sums = lax.all_to_all(by_rows, ZY, split_axis=0, concat_axis=0, tiled=True)

    pick = lambda i, cr: jnp.where(i == 0, cr[0], 1 - cr[0])
    gg, gu, gd, send = pl.pallas_call(
        weight_kernel,
        grid_spec=prefetched(
            (2, 4),
            [
                VMEM,
                VMEM,
                pl.BlockSpec((1, slots, 512), lambda i, j, cr: (pick(i, cr), 0, j)),
                pl.BlockSpec((1, slots, 512), lambda i, j, cr: (pick(i, cr), 0, j)),
            ],
            [pl.BlockSpec((1, f, 512), lambda i, j, cr: (pick(i, cr), 0, 2 * j + cr[0]))] * 3
            + [pl.BlockSpec((1, 3, f, 512), lambda i, j, cr: (pick(i, cr), 0, 0, j))],
            [pltpu.VMEM((6 * f, slots), BF)],
        ),
        out_shape=[like((2, f, width))] * 3 + [like((2, 3, f, half))],
        compiler_params=params(24),
        cost_estimate=cost(4 * slots * half * 6 * f, 24e6),
        name="weights",
    )(cs, mine, theirs, xs, gs)
    r1, r2, r3, gg, gu, gd, send = together(r1, r2, r3, gg, gu, gd, send)
    kept = sum(v.astype(F32) for v in (ring[0], r1, r2, r3)).astype(BF)
    kept = kept.reshape(2, 16, CAP, 256).transpose(1, 0, 2, 3)
    row_sums, kept, gg, gu, gd, send = together(row_sums, kept, gg, gu, gd, send)
    returned = lax.all_to_all(kept, ZY, split_axis=0, concat_axis=0, tiled=True)
    strips = pl.BlockSpec(strip, lambda j, cr: (0, 0, 2 * j + 1 - cr[0]))
    grads = pl.pallas_call(
        settle_kernel,
        grid_spec=prefetched(
            (4,),
            [pl.BlockSpec((2, 3, f, 512), lambda j, cr: (0, 0, 0, j))] + [pl.BlockSpec(memory_space=pl.ANY)] * 3,
            [strips] * 3,
        ),
        out_shape=[like((2, f, width))] * 3,
        input_output_aliases={2: 0, 3: 1, 4: 2},
        cost_estimate=cost(0, 9.4e6),
        name="settle",
    )(cs, swap(send), gg, gu, gd)

    cx = jnp.concatenate([cs, xx])
    sums = pl.pallas_call(
        rows_kernel,
        out_shape=like((4, rows, 256), F32),
        in_specs=[SMEM, VMEM, VMEM],
        out_specs=VMEM,
        compiler_params=params(24),
        cost_estimate=cost(1e9, 6.5e6),
        name="rows",
    )(cx, own, row_sums)
    s1, s2, s3 = shift(sums[1], 1), shift(sums[2], 2), shift(sums[3], -1)
    s1, s2, s3, *grads = together(s1, s2, s3, *grads)
    grad_tokens = pl.pallas_call(
        combine_kernel,
        out_shape=like((rows, 512)),
        in_specs=[SMEM] + [VMEM] * 6,
        out_specs=VMEM,
        compiler_params=params(24),
        cost_estimate=cost(1e9, 6.5e6),
        name="combine",
    )(cx, own, returned, sums[0], s1, s2, s3)
    return (grad_tokens, *grads)


def solution(mesh):
    fine = Mesh(mesh.devices.reshape(4, 4, 4, 2), ("z", "y", "x", "c"))
    rows = P(ZY, None)
    weights = P(ZY, ("x", "c"), None)
    return jax.shard_map(
        shards,
        mesh=fine,
        in_specs=(rows, rows, rows, rows, weights, weights, weights),
        out_specs=(P(ZY, ("x", "c")), weights, weights, weights),
        check_vma=False,
    )
```

```python
import jax
import jax.numpy as jnp
from jax import lax
from jax.experimental import pallas as pl
from jax.experimental.pallas import tpu as pltpu
from jax.sharding import Mesh
from jax.sharding import PartitionSpec as P

BF = jnp.bfloat16
F32 = jnp.float32
CAP = 48
ZY = ("z", "y")
ZYX = ("z", "y", "x")
VMEM = pl.BlockSpec(memory_space=pltpu.VMEM)
SMEM = pl.BlockSpec(memory_space=pltpu.SMEM)
SWAP = [(0, 1), (1, 0)]


def params(mib):
    return pltpu.CompilerParams(vmem_limit_bytes=mib * 1024 * 1024)


def cost(flops, nbytes):
    return pl.CostEstimate(flops=int(flops / 1e3), bytes_accessed=int(nbytes / 1e3), transcendentals=0)


def nt(a, b):
    return lax.dot_general(a, b, (((1,), (1,)), ((), ())), preferred_element_type=F32)


def mm(a, b):
    return jnp.dot(a, b, preferred_element_type=F32)


def swap(v):
    return lax.ppermute(v, "c", SWAP)


def pairs(to):
    spot = lambda z, y, x, c: ((z % 4 * 4 + y % 4) * 4 + x % 4) * 2 + c
    places = [(z, y, x, c) for z in range(4) for y in range(4) for x in range(4) for c in range(2)]
    return [(spot(*p), spot(*to(*p))) for p in places]


def first(s):
    return pairs(lambda z, y, x, c: (z + s, y, x, c) if c == 0 else (z, y + s, x, c))


def second(s):
    return pairs(lambda z, y, x, c: (z, y + s, x, c) if c == 0 else (z + s, y, x, c))


along = pairs(lambda z, y, x, c: (z, y, x + 1 if c == 0 else x - 1, c))


def hop(v, to):
    return lax.ppermute(v, ("z", "y", "x", "c"), to)


def together(*v):
    return lax.optimization_barrier(v)


def like(shape, dtype=BF):
    return jax.ShapeDtypeStruct(shape, dtype)


def prefetched(grid, in_specs, out_specs, scratch=()):
    return pltpu.PrefetchScalarGridSpec(
        num_scalar_prefetch=1, grid=grid, in_specs=in_specs, out_specs=out_specs, scratch_shapes=list(scratch)
    )


def pack_kernel(at_ref, ids_ref, wts_ref, t0, t1, g0, g1, g2, g3, out_ref):
    top, rows = ids_ref.shape
    expert = lax.broadcasted_iota(jnp.int32, (32, rows), 0)
    hit = jnp.zeros((32, rows), F32)
    wt = jnp.zeros((32, rows), F32)
    for k in range(top):
        same = ids_ref[k : k + 1, :] == expert
        hit = hit + same.astype(F32)
        wt = wt + jnp.where(same, wts_ref[k : k + 1, :], 0.0)
    r = lax.broadcasted_iota(jnp.int32, (rows, rows), 0)
    q = lax.broadcasted_iota(jnp.int32, (rows, rows), 1)
    before = mm(hit.astype(BF), (r < q).astype(BF))
    pos = jnp.where(hit > 0.5, before, -1.0)
    high = wt.astype(BF)
    rest = wt - high.astype(F32)
    mid = rest.astype(BF)
    low = (rest - mid.astype(F32)).astype(BF)
    out_ref[:, 0:512] = t0[...]
    out_ref[:, 512:1024] = t1[...]
    out_ref[:, 1024:1152] = jnp.concatenate([pos.astype(BF), high, mid, low], axis=0)
    for i, ref in enumerate((g0, g1, g2, g3)):
        out_ref[:, 1152 + i * 512 : 1664 + i * 512] = ref[...]


def chosen(row):
    p = lax.broadcasted_iota(jnp.int32, (CAP, row.shape[1]), 0).astype(F32)
    return row == p


def outgoing_kernel(c_ref, g_ref, u_ref, d_ref, out_ref):
    out_ref[0:2] = g_ref[...]
    out_ref[2:4] = u_ref[...]
    out_ref[4:6] = d_ref[...]


def assemble_kernel(c_ref, g_ref, u_ref, d_ref, in_ref, wgu_ref, wd_ref):
    f = g_ref.shape[1]

    def place(low, high):
        for e in range(2):
            wgu_ref[e, low : low + f] = g_ref[e]
            wgu_ref[e, high : high + f] = in_ref[e]
            wgu_ref[e, 2 * f + low : 3 * f + low] = u_ref[e]
            wgu_ref[e, 2 * f + high : 3 * f + high] = in_ref[2 + e]
            wd_ref[e, low : low + f] = d_ref[e]
            wd_ref[e, high : high + f] = in_ref[4 + e]

    @pl.when(c_ref[0] == 0)
    def _():
        place(0, f)

    @pl.when(c_ref[0] == 1)
    def _():
        place(f, 0)


def picked(info_ref, meta, held):
    held[...] = meta.astype(F32)
    picks, scales = [], []
    for k in range(2):
        row = info_ref[0] + k
        pick = chosen(held[pl.ds(row, 1), :])
        wt = held[pl.ds(32 + row, 1), :] + held[pl.ds(64 + row, 1), :] + held[pl.ds(96 + row, 1), :]
        picks.append(pick.astype(F32))
        scales.append(jnp.sum(jnp.where(pick, wt, 0.0), axis=1, keepdims=True))
    return jnp.concatenate(picks, axis=0).astype(BF), jnp.concatenate(scales, axis=0)


def select_x_kernel(info_ref, near_ref, far_ref, *rest):
    out_ref, held = rest[-2:]
    w = out_ref.shape[2] // 2
    pick, _ = picked(info_ref, near_ref[0, :, w:], held)
    for i, ref in enumerate((near_ref, far_ref)):
        got = mm(pick, ref[0, :, 0:w]).astype(BF)
        side = info_ref[1] if i == 0 else 1 - info_ref[1]
        cols = pl.ds(pl.multiple_of(side * w, w), w)
        out_ref[0, :, cols] = got[0:CAP]
        out_ref[1, :, cols] = got[CAP:]


def select_g_kernel(info_ref, near_ref, g_ref, *rest):
    out_ref, held = rest[-2:]
    pick, scale = picked(info_ref, near_ref[0], held)
    got = (mm(pick, g_ref[0]) * scale).astype(BF)
    out_ref[0] = got[0:CAP]
    out_ref[1] = got[CAP:]


def hidden_kernel(e_ref, v_ref, w_ref, out_ref):
    out_ref[...] = nt(v_ref[0], w_ref[0])


def act_kernel(a_ref, b_ref, d_ref, e_ref, out_ref):
    n = out_ref.shape[1] // 3
    h = a_ref[...] + b_ref[...]
    gate, up = h[:, 0:n], h[:, n:]
    d = d_ref[...] + e_ref[...]
    sig = jax.nn.sigmoid(gate)
    silu = gate * sig
    out_ref[:, 0:n] = (d * up * sig * (1.0 + gate * (1.0 - sig))).astype(BF)
    out_ref[:, n : 2 * n] = (d * silu).astype(BF)
    out_ref[:, 2 * n :] = (silu * up).astype(BF)


def by_x_kernel(e_ref, ad_ref, wgu_ref, out_ref):
    out_ref[0] = mm(ad_ref[:, 0 : wgu_ref.shape[1]], wgu_ref[0]).astype(BF)


def by_block_kernel(e_ref, ad_ref, wgu_ref, out_ref):
    out_ref[...] = mm(ad_ref[:, 0 : wgu_ref.shape[1]], wgu_ref[0]).astype(BF).reshape(out_ref.shape)


def weight_kernel(c_ref, mine_ref, theirs_ref, xs_ref, gs_ref, gg_ref, gu_ref, gd_ref, send_ref, dt):
    f = gg_ref.shape[1]
    first = pl.program_id(1) == 0

    @pl.when(first & (pl.program_id(0) == 0))
    def _():
        dt[...] = mine_ref[...].astype(F32).T.astype(BF)

    @pl.when(first & (pl.program_id(0) == 1))
    def _():
        dt[...] = theirs_ref[...].astype(F32).T.astype(BF)

    c = c_ref[0]
    outs = (gg_ref, gu_ref, gd_ref)
    for i in range(3):
        rows = xs_ref if i < 2 else gs_ref
        keep = pl.ds(pl.multiple_of(2 * f * i + f * c, f), f)
        away = pl.ds(pl.multiple_of(2 * f * i + f * (1 - c), f), f)
        outs[i][0] = mm(dt[keep, :], rows[0]).astype(BF)
        send_ref[0, i] = mm(dt[away, :], rows[0]).astype(BF)


def settle_kernel(c_ref, in_ref, a_ref, b_ref, d_ref, gg_ref, gu_ref, gd_ref):
    for e in range(2):
        gg_ref[e] = in_ref[e, 0]
        gu_ref[e] = in_ref[e, 1]
        gd_ref[e] = in_ref[e, 2]


def gathering(parity, pw_ref):
    low = parity == 0
    places = pw_ref[0:32, 1024:1152].astype(F32)
    picks = []
    for e in range(16):
        row = jnp.where(low, places[2 * e : 2 * e + 1], places[2 * e + 1 : 2 * e + 2])
        picks.append(chosen(row).astype(F32))
    return jnp.concatenate(picks, axis=0).T.astype(BF)


def rows_kernel(c_ref, pw_ref, ret_ref, out_ref):
    total = mm(gathering(c_ref[0], pw_ref), ret_ref[...].reshape(16 * CAP, 2048)).astype(BF)
    for j in range(4):
        out_ref[lax.rem(j - c_ref[1] + 4, 4)] = total[:, j * 512 : (j + 1) * 512]


def combine_kernel(c_ref, pw_ref, ret_ref, a_ref, b_ref, d_ref, e_ref, out_ref):
    total = mm(gathering(1 - c_ref[0], pw_ref), ret_ref[...].reshape(16 * CAP, 512))
    for ref in (a_ref, b_ref, d_ref, e_ref):
        total = total + ref[...].astype(F32)
    out_ref[...] = total.astype(BF)


def shards(tokens, expert_ids, route_weights, grad_out, w_gate, w_up, w_down):
    rows, width = tokens.shape
    f = w_gate.shape[1]
    slots = 16 * CAP
    half = width // 2
    c = lax.axis_index("c")
    x = lax.axis_index("x")
    cs = jnp.reshape(c, (1,)).astype(jnp.int32)
    others = 1 - cs

    z, y = lax.axis_index("z"), lax.axis_index("y")
    side = x % 2

    piece = lambda k: pl.BlockSpec((rows, 512), lambda i, ar: (0, ar[k]))
    flat = lambda v: pl.BlockSpec(v.shape, lambda i, ar: (0, 0))
    ids, wts = expert_ids.T, route_weights.T
    own = pl.pallas_call(
        pack_kernel,
        grid_spec=prefetched(
            (1,),
            [flat(ids), flat(wts)] + [piece(k) for k in range(6)],
            pl.BlockSpec((rows, 3200), lambda i, ar: (0, 0)),
        ),
        out_shape=like((rows, 3200)),
        cost_estimate=cost(1e7, 2e6),
        name="pack",
    )(
        jnp.stack([2 * k + c for k in (2 * side, 2 * side + 1, 0, 1, 2, 3)]).astype(jnp.int32),
        *(ids, wts, tokens, tokens, grad_out, grad_out, grad_out, grad_out),
    )

    strip = (2, f, 512)
    outgoing = pl.pallas_call(
        outgoing_kernel,
        grid_spec=prefetched(
            (4,),
            [pl.BlockSpec(strip, lambda j, cr: (0, 0, 2 * j + 1 - cr[0]))] * 3,
            pl.BlockSpec((6, f, 512), lambda j, cr: (0, 0, j)),
        ),
        out_shape=like((6, f, half)),
        cost_estimate=cost(0, 9.4e6),
        name="outgoing",
    )(cs, w_gate, w_up, w_down)

    up, down = hop(own, first(1)), hop(own, first(-1))
    up, down, outgoing = together(up, down, outgoing)
    far0, far1, incoming = hop(up[:64], first(1)), hop(down[64:], first(-1)), swap(outgoing)
    far0, far1, incoming = together(far0, far1, incoming)
    far = jnp.concatenate([far0, far1], axis=0)
    line = [own, up, down, far]
    xg = jnp.stack([v[:, :1152] for v in line])
    gg = jnp.stack([v[:, 1152:] for v in line])
    wgu, wd = pl.pallas_call(
        assemble_kernel,
        grid_spec=prefetched(
            (4,),
            [pl.BlockSpec(strip, lambda j, cr: (0, 0, 2 * j + cr[0]))] * 3
            + [pl.BlockSpec((6, f, 512), lambda j, cr: (0, 0, j))],
            [
                pl.BlockSpec((2, 4 * f, 512), lambda j, cr: (0, 0, j)),
                pl.BlockSpec((2, 2 * f, 512), lambda j, cr: (0, 0, j)),
            ],
        ),
        out_shape=(like((2, 4 * f, half)), like((2, 2 * f, half))),
        compiler_params=params(24),
        cost_estimate=cost(0, 19e6),
        name="assemble",
    )(cs, w_gate, w_up, w_down, incoming)
    xm, xr, xg_far = hop(xg, second(1)), hop(xg, second(-1)), hop(xg, along)
    gg, xm, xr, xg_far, wgu, wd = together(gg, xm, xr, xg_far, wgu, wd)
    gm, gr = hop(gg, second(1)), hop(gg, second(-1))
    xd0, xd1 = hop(xm[:2], second(1)), hop(xr[2:], second(-1))
    xm_far = hop(xm, along)

    offsets = (0, -1, 1, 2)
    table = []
    for b in offsets:
        for a in offsets:
            oz, oy = jnp.where(c == 0, a, b), jnp.where(c == 0, b, a)
            table.append((z + oz + 4) % 4 * 4 + (y + oy + 4) % 4)
    info = jnp.stack([2 * (z * 4 + y), side] + table).astype(jnp.int32)

    def select(kernel, start, near, other, into, skip=0):
        is_x = kernel is select_x_kernel
        if is_x:
            specs = [pl.BlockSpec((1, rows, 1152), lambda i, fo: (i, 0, 0))] * 2
        else:
            specs = [
                pl.BlockSpec((1, rows, 128), lambda i, fo: (i + skip, 0, 8)),
                pl.BlockSpec((1, rows, half), lambda i, fo: (i, 0, 0)),
            ]
        n = other.shape[0]
        return pl.pallas_call(
            kernel,
            grid_spec=prefetched(
                (n,),
                specs + [pl.BlockSpec(memory_space=pl.ANY)] * len(into),
                pl.BlockSpec((2, CAP, half), lambda i, fo: (0, fo[2 + start + i], 0)),
                [pltpu.VMEM((rows, rows), F32)],
            ),
            out_shape=like((2, slots, half)),
            input_output_aliases={3: 0} if into else {},
            compiler_params=params(24),
            cost_estimate=cost(2 * n * 2 * CAP * rows * half, n * 1.4e6),
            name="select",
        )(info, near, other, *into)

    xs = select(select_x_kernel, 0, xg, xg_far, [])
    gs = select(select_g_kernel, 0, xg, gg, [])
    xm_far, xr_go, xs, gs = together(xm_far, xr, xs, gs)
    xr_far = hop(xr_go, along)
    xs = select(select_x_kernel, 4, xm, xm_far, [xs])
    gm, gr, xd0, xd1, xr_far, xs = together(gm, gr, xd0, xd1, xr_far, xs)
    gd0, gd1 = hop(gm[:2], second(1)), hop(gr[2:], second(-1))
    xd = jnp.concatenate([xd0, xd1], axis=0)
    xd_far = hop(xd, along)
    gs = select(select_g_kernel, 4, xm, gm, [gs])
    xs = select(select_x_kernel, 8, xr, xr_far, [xs])
    gs = select(select_g_kernel, 8, xr, gr, [gs])
    xs = select(select_x_kernel, 12, xd, xd_far, [xs])
    def hidden(which, v, w, chunk):
        n = w.shape[1]
        return pl.pallas_call(
            hidden_kernel,
            grid_spec=prefetched(
                (n // chunk,),
                [
                    pl.BlockSpec((1, slots, half), lambda j, er: (er[0], 0, 0)),
                    pl.BlockSpec((1, chunk, half), lambda j, er: (er[0], j, 0)),
                ],
                pl.BlockSpec((slots, chunk), lambda j, er: (0, j)),
            ),
            out_shape=like((slots, n), F32),
            compiler_params=params(24),
            cost_estimate=cost(2 * slots * half * n, 9e6),
            name="hidden",
        )(which, v, w)

    pre_out, pre = hidden(others, xs, wgu, 256), hidden(cs, xs, wgu, 256)
    gd0, gd1, gs, pre_out, pre = together(gd0, gd1, gs, pre_out, pre)
    pre_in = swap(pre_out)
    gs = select(select_g_kernel, 12, xd, gd0, [gs])
    gs = select(select_g_kernel, 14, xd, gd1, [gs], 2)
    dh_in = swap(hidden(others, gs, wd, 128))
    dh = hidden(cs, gs, wd, 128)
    quarter = lambda n: pl.BlockSpec((slots // 4, n), lambda j: (j, 0))
    mine = pl.pallas_call(
        act_kernel,
        grid=(4,),
        out_shape=like((slots, 6 * f)),
        in_specs=[quarter(4 * f), quarter(4 * f), quarter(2 * f), quarter(2 * f)],
        out_specs=quarter(6 * f),
        compiler_params=params(24),
        cost_estimate=cost(1e7, 9e6),
        name="act",
    )(pre, pre_in, dh, dh_in)
    theirs = swap(mine)

    def partial(kernel, which, ad):
        if kernel is by_x_kernel:
            shape = (4, slots, 512)
            out = pl.BlockSpec((1, slots, 512), lambda j, er: (lax.rem(j - er[1] + 4, 4), 0, 0))
        else:
            shape = (16, CAP, half)
            out = pl.BlockSpec((16, CAP, 512), lambda j, er: (0, 0, j))
        return pl.pallas_call(
            kernel,
            grid_spec=prefetched(
                (4,), [VMEM, pl.BlockSpec((1, 4 * f, 512), lambda j, er: (er[0], 0, j))], out
            ),
            out_shape=like(shape),
            compiler_params=params(24),
            cost_estimate=cost(2 * slots * half * 4 * f, 8e6),
            name="partial",
        )(jnp.concatenate([which, xx]), ad, wgu)

    shift = lambda v, k: lax.ppermute(v, "x", [(i, (i + k) % 4) for i in range(4)])
    xx = jnp.reshape(x, (1,)).astype(jnp.int32)
    by_block = partial(by_block_kernel, cs, mine)
    row_sums = lax.all_to_all(by_block, ZY, split_axis=0, concat_axis=0, tiled=True)
    by_block, theirs = together(by_block, theirs)
    ring = partial(by_x_kernel, others, theirs)
    ring, mine, theirs = together(ring, mine, theirs)
    r1, r2, r3 = shift(ring[1], 1), shift(ring[2], 2), shift(ring[3], -1)

    pick = lambda i, cr: jnp.where(i == 0, cr[0], 1 - cr[0])
    gg, gu, gd, send = pl.pallas_call(
        weight_kernel,
        grid_spec=prefetched(
            (2, 4),
            [
                VMEM,
                VMEM,
                pl.BlockSpec((1, slots, 512), lambda i, j, cr: (pick(i, cr), 0, j)),
                pl.BlockSpec((1, slots, 512), lambda i, j, cr: (pick(i, cr), 0, j)),
            ],
            [pl.BlockSpec((1, f, 512), lambda i, j, cr: (pick(i, cr), 0, 2 * j + cr[0]))] * 3
            + [pl.BlockSpec((1, 3, f, 512), lambda i, j, cr: (pick(i, cr), 0, 0, j))],
            [pltpu.VMEM((6 * f, slots), BF)],
        ),
        out_shape=[like((2, f, width))] * 3 + [like((2, 3, f, half))],
        compiler_params=params(24),
        cost_estimate=cost(4 * slots * half * 6 * f, 24e6),
        name="weights",
    )(cs, mine, theirs, xs, gs)
    r1, r2, r3, gg, gu, gd, send = together(r1, r2, r3, gg, gu, gd, send)
    kept = sum(v.astype(F32) for v in (ring[0], r1, r2, r3)).astype(BF)
    kept = kept.reshape(16, CAP, 512)
    row_sums, kept, gg, gu, gd, send = together(row_sums, kept, gg, gu, gd, send)
    returned = lax.all_to_all(kept, ZY, split_axis=0, concat_axis=0, tiled=True)
    strips = pl.BlockSpec(strip, lambda j, cr: (0, 0, 2 * j + 1 - cr[0]))
    grads = pl.pallas_call(
        settle_kernel,
        grid_spec=prefetched(
            (4,),
            [pl.BlockSpec((2, 3, f, 512), lambda j, cr: (0, 0, 0, j))] + [pl.BlockSpec(memory_space=pl.ANY)] * 3,
            [strips] * 3,
        ),
        out_shape=[like((2, f, width))] * 3,
        input_output_aliases={2: 0, 3: 1, 4: 2},
        cost_estimate=cost(0, 9.4e6),
        name="settle",
    )(cs, swap(send), gg, gu, gd)

    cx = jnp.concatenate([cs, xx])
    sums = pl.pallas_call(
        rows_kernel,
        out_shape=like((4, rows, 512)),
        in_specs=[SMEM, VMEM, VMEM],
        out_specs=VMEM,
        compiler_params=params(24),
        cost_estimate=cost(1e9, 6.5e6),
        name="rows",
    )(cx, own, row_sums)
    s1, s2, s3 = shift(sums[1], 1), shift(sums[2], 2), shift(sums[3], -1)
    s1, s2, s3, *grads = together(s1, s2, s3, *grads)
    grad_tokens = pl.pallas_call(
        combine_kernel,
        out_shape=like((rows, 512)),
        in_specs=[SMEM] + [VMEM] * 6,
        out_specs=VMEM,
        compiler_params=params(24),
        cost_estimate=cost(1e9, 6.5e6),
        name="combine",
    )(cx, own, returned, sums[0], s1, s2, s3)
    return (grad_tokens, *grads)


def solution(mesh):
    fine = Mesh(mesh.devices.reshape(4, 4, 4, 2), ("z", "y", "x", "c"))
    rows = P(ZY, None)
    weights = P(ZY, ("x", "c"), None)
    return jax.shard_map(
        shards,
        mesh=fine,
        in_specs=(rows, rows, rows, rows, weights, weights, weights),
        out_specs=(P(ZY, ("x", "c")), weights, weights, weights),
        check_vma=False,
    )
```

```python
import jax
import jax.numpy as jnp
from jax import lax
from jax.experimental import pallas as pl
from jax.experimental.pallas import tpu as pltpu
from jax.sharding import Mesh
from jax.sharding import PartitionSpec as P

BF = jnp.bfloat16
F32 = jnp.float32
CAP = 48
ZY = ("z", "y")
ZYX = ("z", "y", "x")
VMEM = pl.BlockSpec(memory_space=pltpu.VMEM)
SMEM = pl.BlockSpec(memory_space=pltpu.SMEM)
SWAP = [(0, 1), (1, 0)]


def params(mib):
    return pltpu.CompilerParams(vmem_limit_bytes=mib * 1024 * 1024)


def cost(flops, nbytes):
    return pl.CostEstimate(flops=int(flops / 1e3), bytes_accessed=int(nbytes / 1e3), transcendentals=0)


def nt(a, b):
    return lax.dot_general(a, b, (((1,), (1,)), ((), ())), preferred_element_type=F32)


def mm(a, b):
    return jnp.dot(a, b, preferred_element_type=F32)


def swap(v):
    return lax.ppermute(v, "c", SWAP)


def pairs(to):
    spot = lambda z, y, x, c: ((z % 4 * 4 + y % 4) * 4 + x % 4) * 2 + c
    places = [(z, y, x, c) for z in range(4) for y in range(4) for x in range(4) for c in range(2)]
    return [(spot(*p), spot(*to(*p))) for p in places]


def first(s):
    return pairs(lambda z, y, x, c: (z + s, y, x, c) if c == 0 else (z, y + s, x, c))


def second(s):
    return pairs(lambda z, y, x, c: (z, y + s, x, c) if c == 0 else (z + s, y, x, c))


along = pairs(lambda z, y, x, c: (z, y, x + 1 if c == 0 else x - 1, c))


def hop(v, to):
    return lax.ppermute(v, ("z", "y", "x", "c"), to)


def together(*v):
    return lax.optimization_barrier(v)


def like(shape, dtype=BF):
    return jax.ShapeDtypeStruct(shape, dtype)


def prefetched(grid, in_specs, out_specs, scratch=()):
    return pltpu.PrefetchScalarGridSpec(
        num_scalar_prefetch=1, grid=grid, in_specs=in_specs, out_specs=out_specs, scratch_shapes=list(scratch)
    )


def pack_kernel(at_ref, ids_ref, wts_ref, t0, t1, g0, g1, g2, g3, out_ref):
    top, rows = ids_ref.shape
    expert = lax.broadcasted_iota(jnp.int32, (32, rows), 0)
    hit = jnp.zeros((32, rows), F32)
    wt = jnp.zeros((32, rows), F32)
    for k in range(top):
        same = ids_ref[k : k + 1, :] == expert
        hit = hit + same.astype(F32)
        wt = wt + jnp.where(same, wts_ref[k : k + 1, :], 0.0)
    r = lax.broadcasted_iota(jnp.int32, (rows, rows), 0)
    q = lax.broadcasted_iota(jnp.int32, (rows, rows), 1)
    before = mm(hit.astype(BF), (r < q).astype(BF))
    pos = jnp.where(hit > 0.5, before, -1.0)
    high = wt.astype(BF)
    rest = wt - high.astype(F32)
    mid = rest.astype(BF)
    low = (rest - mid.astype(F32)).astype(BF)
    out_ref[:, 0:512] = t0[...]
    out_ref[:, 512:1024] = t1[...]
    out_ref[:, 1024:1152] = jnp.concatenate([pos.astype(BF), high, mid, low], axis=0)
    for i, ref in enumerate((g0, g1, g2, g3)):
        out_ref[:, 1152 + i * 512 : 1664 + i * 512] = ref[...]


def chosen(row):
    p = lax.broadcasted_iota(jnp.int32, (CAP, row.shape[1]), 0).astype(F32)
    return row == p


def outgoing_kernel(c_ref, g_ref, u_ref, d_ref, out_ref):
    out_ref[0:2] = g_ref[...]
    out_ref[2:4] = u_ref[...]
    out_ref[4:6] = d_ref[...]


def assemble_kernel(c_ref, g_ref, u_ref, d_ref, in_ref, wgu_ref, wd_ref):
    f = g_ref.shape[1]

    def place(low, high):
        for e in range(2):
            wgu_ref[e, low : low + f] = g_ref[e]
            wgu_ref[e, high : high + f] = in_ref[e]
            wgu_ref[e, 2 * f + low : 3 * f + low] = u_ref[e]
            wgu_ref[e, 2 * f + high : 3 * f + high] = in_ref[2 + e]
            wd_ref[e, low : low + f] = d_ref[e]
            wd_ref[e, high : high + f] = in_ref[4 + e]

    @pl.when(c_ref[0] == 0)
    def _():
        place(0, f)

    @pl.when(c_ref[0] == 1)
    def _():
        place(f, 0)


def picked(info_ref, meta, held):
    held[...] = meta.astype(F32)
    picks, scales = [], []
    for k in range(2):
        row = info_ref[0] + k
        pick = chosen(held[pl.ds(row, 1), :])
        wt = held[pl.ds(32 + row, 1), :] + held[pl.ds(64 + row, 1), :] + held[pl.ds(96 + row, 1), :]
        picks.append(pick.astype(F32))
        scales.append(jnp.sum(jnp.where(pick, wt, 0.0), axis=1, keepdims=True))
    return jnp.concatenate(picks, axis=0).astype(BF), jnp.concatenate(scales, axis=0)


def select_x_kernel(info_ref, near_ref, far_ref, *rest):
    out_ref, held = rest[-2:]
    w = out_ref.shape[2] // 2
    pick, _ = picked(info_ref, near_ref[0, :, w:], held)
    for i, ref in enumerate((near_ref, far_ref)):
        got = mm(pick, ref[0, :, 0:w]).astype(BF)
        side = info_ref[1] if i == 0 else 1 - info_ref[1]
        cols = pl.ds(pl.multiple_of(side * w, w), w)
        out_ref[0, :, cols] = got[0:CAP]
        out_ref[1, :, cols] = got[CAP:]


def select_g_kernel(info_ref, near_ref, g_ref, *rest):
    out_ref, held = rest[-2:]
    pick, scale = picked(info_ref, near_ref[0], held)
    got = (mm(pick, g_ref[0]) * scale).astype(BF)
    out_ref[0] = got[0:CAP]
    out_ref[1] = got[CAP:]


def hidden_kernel(e_ref, v_ref, w_ref, out_ref):
    out_ref[...] = nt(v_ref[0], w_ref[0])


def act_kernel(e_ref, v_ref, w_ref, d_ref, g0_ref, g1_ref, u0_ref, u1_ref, out_ref):
    n = out_ref.shape[1] // 3
    d = nt(v_ref[0], w_ref[0]) + d_ref[...]
    gate, up = g0_ref[...] + g1_ref[...], u0_ref[...] + u1_ref[...]
    sig = jax.nn.sigmoid(gate)
    silu = gate * sig
    outs = (d * up * sig * (1.0 + gate * (1.0 - sig)), d * silu, silu * up)
    for i, value in enumerate(outs):
        at = pl.multiple_of(i * n + pl.program_id(0) * 128, 128)
        out_ref[:, pl.ds(at, 128)] = value.astype(BF)


def by_x_kernel(e_ref, ad_ref, wgu_ref, out_ref):
    out_ref[0] = mm(ad_ref[:, 0 : wgu_ref.shape[1]], wgu_ref[0]).astype(BF)


def by_block_kernel(e_ref, ad_ref, wgu_ref, out_ref, stage, sems):
    step = pl.program_id(0)
    turn = lax.rem(step, 2)

    def leaving(j, slot):
        cols = pl.ds(pl.multiple_of(j * 512, 512), 512)
        return pltpu.make_async_copy(stage.at[slot], out_ref.at[:, :, cols], sems.at[slot])

    @pl.when(step >= 2)
    def _():
        leaving(step - 2, turn).wait()

    got = mm(ad_ref[:, 0 : wgu_ref.shape[1]], wgu_ref[0]).astype(BF)
    stage[turn] = got.reshape(stage.shape[1:])
    leaving(step, turn).start()

    @pl.when(step == 3)
    def _():
        leaving(2, 0).wait()
        leaving(3, 1).wait()


def weight_kernel(c_ref, mine_ref, theirs_ref, xs_ref, gs_ref, gg_ref, gu_ref, gd_ref, send_ref, dt):
    f = gg_ref.shape[1]
    first = pl.program_id(1) == 0

    @pl.when(first & (pl.program_id(0) == 0))
    def _():
        dt[...] = mine_ref[...].astype(F32).T.astype(BF)

    @pl.when(first & (pl.program_id(0) == 1))
    def _():
        dt[...] = theirs_ref[...].astype(F32).T.astype(BF)

    c = c_ref[0]
    outs = (gg_ref, gu_ref, gd_ref)
    for i in range(3):
        rows = xs_ref if i < 2 else gs_ref
        keep = pl.ds(pl.multiple_of(2 * f * i + f * c, f), f)
        away = pl.ds(pl.multiple_of(2 * f * i + f * (1 - c), f), f)
        outs[i][0] = mm(dt[keep, :], rows[0]).astype(BF)
        send_ref[0, i] = mm(dt[away, :], rows[0]).astype(BF)


def settle_kernel(c_ref, in_ref, a_ref, b_ref, d_ref, gg_ref, gu_ref, gd_ref):
    for e in range(2):
        gg_ref[e] = in_ref[e, 0]
        gu_ref[e] = in_ref[e, 1]
        gd_ref[e] = in_ref[e, 2]


def gathering(parity, pw_ref):
    low = parity == 0
    places = pw_ref[0:32, 1024:1152].astype(F32)
    picks = []
    for e in range(16):
        row = jnp.where(low, places[2 * e : 2 * e + 1], places[2 * e + 1 : 2 * e + 2])
        picks.append(chosen(row).astype(F32))
    return jnp.concatenate(picks, axis=0).T.astype(BF)


def rows_kernel(c_ref, pw_ref, ret_ref, out_ref):
    total = mm(gathering(c_ref[0], pw_ref), ret_ref[...].reshape(16 * CAP, 2048)).astype(BF)
    for j in range(4):
        out_ref[lax.rem(j - c_ref[1] + 4, 4)] = total[:, j * 512 : (j + 1) * 512]


def combine_kernel(c_ref, pw_ref, ret_ref, a_ref, b_ref, d_ref, e_ref, out_ref):
    total = mm(gathering(1 - c_ref[0], pw_ref), ret_ref[...].reshape(16 * CAP, 512))
    for ref in (a_ref, b_ref, d_ref, e_ref):
        total = total + ref[...].astype(F32)
    out_ref[...] = total.astype(BF)


def shards(tokens, expert_ids, route_weights, grad_out, w_gate, w_up, w_down):
    rows, width = tokens.shape
    f = w_gate.shape[1]
    slots = 16 * CAP
    half = width // 2
    c = lax.axis_index("c")
    x = lax.axis_index("x")
    cs = jnp.reshape(c, (1,)).astype(jnp.int32)
    others = 1 - cs

    z, y = lax.axis_index("z"), lax.axis_index("y")
    side = x % 2

    piece = lambda k: pl.BlockSpec((rows, 512), lambda i, ar: (0, ar[k]))
    flat = lambda v: pl.BlockSpec(v.shape, lambda i, ar: (0, 0))
    ids, wts = expert_ids.T, route_weights.T
    own = pl.pallas_call(
        pack_kernel,
        grid_spec=prefetched(
            (1,),
            [flat(ids), flat(wts)] + [piece(k) for k in range(6)],
            pl.BlockSpec((rows, 3200), lambda i, ar: (0, 0)),
        ),
        out_shape=like((rows, 3200)),
        cost_estimate=cost(1e7, 2e6),
        name="pack",
    )(
        jnp.stack([2 * k + c for k in (2 * side, 2 * side + 1, 0, 1, 2, 3)]).astype(jnp.int32),
        *(ids, wts, tokens, tokens, grad_out, grad_out, grad_out, grad_out),
    )

    strip = (2, f, 512)
    outgoing = pl.pallas_call(
        outgoing_kernel,
        grid_spec=prefetched(
            (4,),
            [pl.BlockSpec(strip, lambda j, cr: (0, 0, 2 * j + 1 - cr[0]))] * 3,
            pl.BlockSpec((6, f, 512), lambda j, cr: (0, 0, j)),
        ),
        out_shape=like((6, f, half)),
        cost_estimate=cost(0, 9.4e6),
        name="outgoing",
    )(cs, w_gate, w_up, w_down)

    up, down = hop(own, first(1)), hop(own, first(-1))
    up, down, outgoing = together(up, down, outgoing)
    far0, far1, incoming = hop(up[:64], first(1)), hop(down[64:], first(-1)), swap(outgoing)
    far0, far1, incoming = together(far0, far1, incoming)
    far = jnp.concatenate([far0, far1], axis=0)
    line = [own, up, down, far]
    xg = jnp.stack([v[:, :1152] for v in line])
    gg = jnp.stack([v[:, 1152:] for v in line])
    wgu, wd = pl.pallas_call(
        assemble_kernel,
        grid_spec=prefetched(
            (4,),
            [pl.BlockSpec(strip, lambda j, cr: (0, 0, 2 * j + cr[0]))] * 3
            + [pl.BlockSpec((6, f, 512), lambda j, cr: (0, 0, j))],
            [
                pl.BlockSpec((2, 4 * f, 512), lambda j, cr: (0, 0, j)),
                pl.BlockSpec((2, 2 * f, 512), lambda j, cr: (0, 0, j)),
            ],
        ),
        out_shape=(like((2, 4 * f, half)), like((2, 2 * f, half))),
        compiler_params=params(24),
        cost_estimate=cost(0, 19e6),
        name="assemble",
    )(cs, w_gate, w_up, w_down, incoming)
    xm, xr, xg_far = hop(xg, second(1)), hop(xg, second(-1)), hop(xg, along)
    gg, xm, xr, xg_far, wgu, wd = together(gg, xm, xr, xg_far, wgu, wd)
    gm, gr = hop(gg, second(1)), hop(gg, second(-1))
    xd0, xd1 = hop(xm[:2], second(1)), hop(xr[2:], second(-1))
    xm_far = hop(xm, along)

    offsets = (0, -1, 1, 2)
    table = []
    for b in offsets:
        for a in offsets:
            oz, oy = jnp.where(c == 0, a, b), jnp.where(c == 0, b, a)
            table.append((z + oz + 4) % 4 * 4 + (y + oy + 4) % 4)
    info = jnp.stack([2 * (z * 4 + y), side] + table).astype(jnp.int32)

    def select(kernel, start, near, other, into, skip=0):
        is_x = kernel is select_x_kernel
        if is_x:
            specs = [pl.BlockSpec((1, rows, 1152), lambda i, fo: (i, 0, 0))] * 2
        else:
            specs = [
                pl.BlockSpec((1, rows, 128), lambda i, fo: (i + skip, 0, 8)),
                pl.BlockSpec((1, rows, half), lambda i, fo: (i, 0, 0)),
            ]
        n = other.shape[0]
        return pl.pallas_call(
            kernel,
            grid_spec=prefetched(
                (n,),
                specs + [pl.BlockSpec(memory_space=pl.ANY)] * len(into),
                pl.BlockSpec((2, CAP, half), lambda i, fo: (0, fo[2 + start + i], 0)),
                [pltpu.VMEM((rows, rows), F32)],
            ),
            out_shape=like((2, slots, half)),
            input_output_aliases={3: 0} if into else {},
            compiler_params=params(24),
            cost_estimate=cost(2 * n * 2 * CAP * rows * half, n * 1.4e6),
            name="select",
        )(info, near, other, *into)

    xs = select(select_x_kernel, 0, xg, xg_far, [])
    gs = select(select_g_kernel, 0, xg, gg, [])
    xm_far, xr_go, xs, gs = together(xm_far, xr, xs, gs)
    xr_far = hop(xr_go, along)
    xs = select(select_x_kernel, 4, xm, xm_far, [xs])
    gm, gr, xd0, xd1, xr_far, xs = together(gm, gr, xd0, xd1, xr_far, xs)
    gd0, gd1 = hop(gm[:2], second(1)), hop(gr[2:], second(-1))
    xd = jnp.concatenate([xd0, xd1], axis=0)
    xd_far = hop(xd, along)
    gs = select(select_g_kernel, 4, xm, gm, [gs])
    xs = select(select_x_kernel, 8, xr, xr_far, [xs])
    gs = select(select_g_kernel, 8, xr, gr, [gs])
    xs = select(select_x_kernel, 12, xd, xd_far, [xs])
    def hidden(which, v, w, chunk):
        n = w.shape[1]
        return pl.pallas_call(
            hidden_kernel,
            grid_spec=prefetched(
                (n // chunk,),
                [
                    pl.BlockSpec((1, slots, half), lambda j, er: (er[0], 0, 0)),
                    pl.BlockSpec((1, chunk, half), lambda j, er: (er[0], j, 0)),
                ],
                pl.BlockSpec((slots, chunk), lambda j, er: (0, j)),
            ),
            out_shape=like((slots, n), F32),
            compiler_params=params(24),
            cost_estimate=cost(2 * slots * half * n, 9e6),
            name="hidden",
        )(which, v, w)

    pre_out = hidden(others, xs, wgu, 256)
    gd0, gd1, gs, pre_out = together(gd0, gd1, gs, pre_out)
    pre_in = swap(pre_out)
    gs = select(select_g_kernel, 12, xd, gd0, [gs])
    gs = select(select_g_kernel, 14, xd, gd1, [gs], 2)
    dh_out = hidden(others, gs, wd, 128)
    xs, dh_out = together(xs, dh_out)
    dh_in = swap(dh_out)
    pre = hidden(cs, xs, wgu, 256)
    column = lambda k: pl.BlockSpec((slots, 128), lambda j, er: (0, k + j))
    mine = pl.pallas_call(
        act_kernel,
        grid_spec=prefetched(
            (3,),
            [
                pl.BlockSpec((1, slots, half), lambda j, er: (er[0], 0, 0)),
                pl.BlockSpec((1, 128, half), lambda j, er: (er[0], j, 0)),
                column(0),
                column(0),
                column(0),
                column(3),
                column(3),
            ],
            pl.BlockSpec((slots, 6 * f), lambda j, er: (0, 0)),
        ),
        out_shape=like((slots, 6 * f)),
        compiler_params=params(24),
        cost_estimate=cost(2 * slots * half * 2 * f, 9e6),
        name="act",
    )(cs, gs, wd, dh_in, pre, pre_in, pre, pre_in)
    theirs = swap(mine)

    def partial(kernel, which, ad):
        scratch = []
        if kernel is by_x_kernel:
            shape = like((4, slots, 512))
            out = pl.BlockSpec((1, slots, 512), lambda j, er: (lax.rem(j - er[1] + 4, 4), 0, 0))
        else:
            shape = pltpu.HBM((16, CAP, half), BF)
            out = pl.BlockSpec(memory_space=pltpu.HBM)
            scratch = [pltpu.VMEM((2, 16, CAP, 512), BF), pltpu.SemaphoreType.DMA((2,))]
        return pl.pallas_call(
            kernel,
            grid_spec=prefetched(
                (4,), [VMEM, pl.BlockSpec((1, 4 * f, 512), lambda j, er: (er[0], 0, j))], out, scratch
            ),
            out_shape=shape,
            compiler_params=params(24),
            cost_estimate=cost(2 * slots * half * 4 * f, 8e6),
            name="partial",
        )(jnp.concatenate([which, xx]), ad, wgu)

    shift = lambda v, k: lax.ppermute(v, "x", [(i, (i + k) % 4) for i in range(4)])
    xx = jnp.reshape(x, (1,)).astype(jnp.int32)
    by_block = partial(by_block_kernel, cs, mine)
    row_sums = lax.all_to_all(by_block, ZY, split_axis=0, concat_axis=0, tiled=True)
    by_block, theirs = together(by_block, theirs)
    ring = partial(by_x_kernel, others, theirs)
    ring, mine, theirs = together(ring, mine, theirs)
    r1, r2, r3 = shift(ring[1], 1), shift(ring[2], 2), shift(ring[3], -1)

    pick = lambda i, cr: jnp.where(i == 0, cr[0], 1 - cr[0])
    gg, gu, gd, send = pl.pallas_call(
        weight_kernel,
        grid_spec=prefetched(
            (2, 4),
            [
                VMEM,
                VMEM,
                pl.BlockSpec((1, slots, 512), lambda i, j, cr: (pick(i, cr), 0, j)),
                pl.BlockSpec((1, slots, 512), lambda i, j, cr: (pick(i, cr), 0, j)),
            ],
            [pl.BlockSpec((1, f, 512), lambda i, j, cr: (pick(i, cr), 0, 2 * j + cr[0]))] * 3
            + [pl.BlockSpec((1, 3, f, 512), lambda i, j, cr: (pick(i, cr), 0, 0, j))],
            [pltpu.VMEM((6 * f, slots), BF)],
        ),
        out_shape=[like((2, f, width))] * 3 + [like((2, 3, f, half))],
        compiler_params=params(58),
        cost_estimate=cost(4 * slots * half * 6 * f, 24e6),
        name="weights",
    )(cs, mine, theirs, xs, gs)
    r1, r2, r3, gg, gu, gd, send = together(r1, r2, r3, gg, gu, gd, send)
    kept = sum(v.astype(F32) for v in (ring[0], r1, r2, r3)).astype(BF)
    kept = kept.reshape(16, CAP, 512)
    row_sums, kept, gg, gu, gd, send = together(row_sums, kept, gg, gu, gd, send)
    returned = lax.all_to_all(kept, ZY, split_axis=0, concat_axis=0, tiled=True)
    strips = pl.BlockSpec(strip, lambda j, cr: (0, 0, 2 * j + 1 - cr[0]))
    grads = pl.pallas_call(
        settle_kernel,
        grid_spec=prefetched(
            (4,),
            [pl.BlockSpec((2, 3, f, 512), lambda j, cr: (0, 0, 0, j))] + [pl.BlockSpec(memory_space=pl.ANY)] * 3,
            [strips] * 3,
        ),
        out_shape=[like((2, f, width))] * 3,
        input_output_aliases={2: 0, 3: 1, 4: 2},
        cost_estimate=cost(0, 9.4e6),
        name="settle",
    )(cs, swap(send), gg, gu, gd)

    cx = jnp.concatenate([cs, xx])
    sums = pl.pallas_call(
        rows_kernel,
        out_shape=like((4, rows, 512)),
        in_specs=[SMEM, VMEM, VMEM],
        out_specs=VMEM,
        compiler_params=params(24),
        cost_estimate=cost(1e9, 6.5e6),
        name="rows",
    )(cx, own, row_sums)
    s1, s2, s3 = shift(sums[1], 1), shift(sums[2], 2), shift(sums[3], -1)
    s1, s2, s3, *grads = together(s1, s2, s3, *grads)
    grad_tokens = pl.pallas_call(
        combine_kernel,
        out_shape=like((rows, 512)),
        in_specs=[SMEM] + [VMEM] * 6,
        out_specs=VMEM,
        compiler_params=params(24),
        cost_estimate=cost(1e9, 6.5e6),
        name="combine",
    )(cx, own, returned, sums[0], s1, s2, s3)
    return (grad_tokens, *grads)


def solution(mesh):
    fine = Mesh(mesh.devices.reshape(4, 4, 4, 2), ("z", "y", "x", "c"))
    rows = P(ZY, None)
    weights = P(ZY, ("x", "c"), None)
    return jax.shard_map(
        shards,
        mesh=fine,
        in_specs=(rows, rows, rows, rows, weights, weights, weights),
        out_specs=(P(ZY, ("x", "c")), weights, weights, weights),
        check_vma=False,
    )
```

```python
import jax
import jax.numpy as jnp
from jax import lax
from jax.experimental import pallas as pl
from jax.experimental.pallas import tpu as pltpu
from jax.sharding import Mesh
from jax.sharding import PartitionSpec as P

BF = jnp.bfloat16
F32 = jnp.float32
CAP = 48
ZY = ("z", "y")
ZYX = ("z", "y", "x")
VMEM = pl.BlockSpec(memory_space=pltpu.VMEM)
SMEM = pl.BlockSpec(memory_space=pltpu.SMEM)
SWAP = [(0, 1), (1, 0)]


def params(mib):
    return pltpu.CompilerParams(vmem_limit_bytes=mib * 1024 * 1024)


def cost(flops, nbytes):
    return pl.CostEstimate(flops=int(flops / 1e3), bytes_accessed=int(nbytes / 1e3), transcendentals=0)


def nt(a, b):
    return lax.dot_general(a, b, (((1,), (1,)), ((), ())), preferred_element_type=F32)


def mm(a, b):
    return jnp.dot(a, b, preferred_element_type=F32)


def swap(v):
    return lax.ppermute(v, "c", SWAP)


def pairs(to):
    spot = lambda z, y, x, c: ((z % 4 * 4 + y % 4) * 4 + x % 4) * 2 + c
    places = [(z, y, x, c) for z in range(4) for y in range(4) for x in range(4) for c in range(2)]
    return [(spot(*p), spot(*to(*p))) for p in places]


def first(s):
    return pairs(lambda z, y, x, c: (z + s, y, x, c) if c == 0 else (z, y + s, x, c))


def second(s):
    return pairs(lambda z, y, x, c: (z, y + s, x, c) if c == 0 else (z + s, y, x, c))


along = pairs(lambda z, y, x, c: (z, y, x + 1 if c == 0 else x - 1, c))


def hop(v, to):
    return lax.ppermute(v, ("z", "y", "x", "c"), to)


def together(*v):
    return lax.optimization_barrier(v)


def like(shape, dtype=BF):
    return jax.ShapeDtypeStruct(shape, dtype)


def prefetched(grid, in_specs, out_specs, scratch=()):
    return pltpu.PrefetchScalarGridSpec(
        num_scalar_prefetch=1, grid=grid, in_specs=in_specs, out_specs=out_specs, scratch_shapes=list(scratch)
    )


def pack_kernel(at_ref, ids_ref, wts_ref, t0, t1, g0, g1, g2, g3, out_ref):
    top, rows = ids_ref.shape
    expert = lax.broadcasted_iota(jnp.int32, (32, rows), 0)
    hit = jnp.zeros((32, rows), F32)
    wt = jnp.zeros((32, rows), F32)
    for k in range(top):
        same = ids_ref[k : k + 1, :] == expert
        hit = hit + same.astype(F32)
        wt = wt + jnp.where(same, wts_ref[k : k + 1, :], 0.0)
    r = lax.broadcasted_iota(jnp.int32, (rows, rows), 0)
    q = lax.broadcasted_iota(jnp.int32, (rows, rows), 1)
    before = mm(hit.astype(BF), (r < q).astype(BF))
    pos = jnp.where(hit > 0.5, before, -1.0)
    high = wt.astype(BF)
    rest = wt - high.astype(F32)
    mid = rest.astype(BF)
    low = (rest - mid.astype(F32)).astype(BF)
    out_ref[:, 0:512] = t0[...]
    out_ref[:, 512:1024] = t1[...]
    out_ref[:, 1024:1152] = jnp.concatenate([pos.astype(BF), high, mid, low], axis=0)
    for i, ref in enumerate((g0, g1, g2, g3)):
        out_ref[:, 1152 + i * 512 : 1664 + i * 512] = ref[...]


def chosen(row):
    p = lax.broadcasted_iota(jnp.int32, (CAP, row.shape[1]), 0).astype(F32)
    return row == p


def outgoing_kernel(c_ref, g_ref, u_ref, d_ref, out_ref):
    out_ref[0:2] = g_ref[...]
    out_ref[2:4] = u_ref[...]
    out_ref[4:6] = d_ref[...]


def assemble_kernel(c_ref, g_ref, u_ref, d_ref, in_ref, wgu_ref, wd_ref):
    f = g_ref.shape[1]

    def place(low, high):
        for e in range(2):
            wgu_ref[e, low : low + f] = g_ref[e]
            wgu_ref[e, high : high + f] = in_ref[e]
            wgu_ref[e, 2 * f + low : 3 * f + low] = u_ref[e]
            wgu_ref[e, 2 * f + high : 3 * f + high] = in_ref[2 + e]
            wd_ref[e, low : low + f] = d_ref[e]
            wd_ref[e, high : high + f] = in_ref[4 + e]

    @pl.when(c_ref[0] == 0)
    def _():
        place(0, f)

    @pl.when(c_ref[0] == 1)
    def _():
        place(f, 0)


def picked(info_ref, meta, held):
    held[...] = meta.astype(F32)
    picks, scales = [], []
    for k in range(2):
        row = info_ref[0] + k
        pick = chosen(held[pl.ds(row, 1), :])
        wt = held[pl.ds(32 + row, 1), :] + held[pl.ds(64 + row, 1), :] + held[pl.ds(96 + row, 1), :]
        picks.append(pick.astype(F32))
        scales.append(jnp.sum(jnp.where(pick, wt, 0.0), axis=1, keepdims=True))
    return jnp.concatenate(picks, axis=0).astype(BF), jnp.concatenate(scales, axis=0)


def select_x_kernel(info_ref, near_ref, far_ref, *rest):
    out_ref, held = rest[-2:]
    w = out_ref.shape[2] // 2
    pick, _ = picked(info_ref, near_ref[0, :, w:], held)
    for i, ref in enumerate((near_ref, far_ref)):
        got = mm(pick, ref[0, :, 0:w]).astype(BF)
        side = info_ref[1] if i == 0 else 1 - info_ref[1]
        cols = pl.ds(pl.multiple_of(side * w, w), w)
        out_ref[0, :, cols] = got[0:CAP]
        out_ref[1, :, cols] = got[CAP:]


def select_g_kernel(info_ref, near_ref, g_ref, *rest):
    out_ref, held = rest[-2:]
    pick, scale = picked(info_ref, near_ref[0], held)
    got = (mm(pick, g_ref[0]) * scale).astype(BF)
    out_ref[0] = got[0:CAP]
    out_ref[1] = got[CAP:]


def hidden_kernel(e_ref, v_ref, w_ref, out_ref):
    out_ref[...] = nt(v_ref[0], w_ref[0])


def act_kernel(e_ref, v_ref, w_ref, d_ref, g0_ref, g1_ref, u0_ref, u1_ref, out_ref):
    n = out_ref.shape[1] // 3
    d = nt(v_ref[0], w_ref[0]) + d_ref[...]
    gate, up = g0_ref[...] + g1_ref[...], u0_ref[...] + u1_ref[...]
    sig = jax.nn.sigmoid(gate)
    silu = gate * sig
    outs = (d * up * sig * (1.0 + gate * (1.0 - sig)), d * silu, silu * up)
    for i, value in enumerate(outs):
        out_ref[:, i * n : (i + 1) * n] = value.astype(BF)


def by_x_kernel(e_ref, ad_ref, wgu_ref, out_ref):
    out_ref[0] = mm(ad_ref[:, 0 : wgu_ref.shape[1]], wgu_ref[0]).astype(BF)


def by_block_kernel(e_ref, ad_ref, wgu_ref, out_ref, stage, sems):
    step = pl.program_id(0)
    turn = lax.rem(step, 2)

    def leaving(j, slot):
        cols = pl.ds(pl.multiple_of(j * 512, 512), 512)
        return pltpu.make_async_copy(stage.at[slot], out_ref.at[:, :, cols], sems.at[slot])

    @pl.when(step >= 2)
    def _():
        leaving(step - 2, turn).wait()

    got = mm(ad_ref[:, 0 : wgu_ref.shape[1]], wgu_ref[0]).astype(BF)
    stage[turn] = got.reshape(stage.shape[1:])
    leaving(step, turn).start()

    @pl.when(step == 3)
    def _():
        leaving(2, 0).wait()
        leaving(3, 1).wait()


def weight_kernel(c_ref, mine_ref, theirs_ref, xs_ref, gs_ref, gg_ref, gu_ref, gd_ref, send_ref, dt):
    f = gg_ref.shape[1]
    first = pl.program_id(1) == 0

    @pl.when(first & (pl.program_id(0) == 0))
    def _():
        dt[...] = mine_ref[...].astype(F32).T.astype(BF)

    @pl.when(first & (pl.program_id(0) == 1))
    def _():
        dt[...] = theirs_ref[...].astype(F32).T.astype(BF)

    c = c_ref[0]
    outs = (gg_ref, gu_ref, gd_ref)
    for i in range(3):
        rows = xs_ref if i < 2 else gs_ref
        keep = pl.ds(pl.multiple_of(2 * f * i + f * c, f), f)
        away = pl.ds(pl.multiple_of(2 * f * i + f * (1 - c), f), f)
        outs[i][0] = mm(dt[keep, :], rows[0]).astype(BF)
        send_ref[0, i] = mm(dt[away, :], rows[0]).astype(BF)


def settle_kernel(c_ref, in_ref, a_ref, b_ref, d_ref, gg_ref, gu_ref, gd_ref):
    for e in range(2):
        gg_ref[e] = in_ref[e, 0]
        gu_ref[e] = in_ref[e, 1]
        gd_ref[e] = in_ref[e, 2]


def gathering(parity, pw_ref):
    low = parity == 0
    places = pw_ref[0:32, 1024:1152].astype(F32)
    picks = []
    for e in range(16):
        row = jnp.where(low, places[2 * e : 2 * e + 1], places[2 * e + 1 : 2 * e + 2])
        picks.append(chosen(row).astype(F32))
    return jnp.concatenate(picks, axis=0).T.astype(BF)


def rows_kernel(c_ref, pw_ref, ret_ref, out_ref):
    total = mm(gathering(c_ref[0], pw_ref), ret_ref[...].reshape(16 * CAP, 2048)).astype(BF)
    for j in range(4):
        out_ref[lax.rem(j - c_ref[1] + 4, 4)] = total[:, j * 512 : (j + 1) * 512]


def combine_kernel(c_ref, pw_ref, ret_ref, a_ref, b_ref, d_ref, e_ref, out_ref):
    total = mm(gathering(1 - c_ref[0], pw_ref), ret_ref[...].reshape(16 * CAP, 512))
    for ref in (a_ref, b_ref, d_ref, e_ref):
        total = total + ref[...].astype(F32)
    out_ref[...] = total.astype(BF)


def shards(tokens, expert_ids, route_weights, grad_out, w_gate, w_up, w_down):
    rows, width = tokens.shape
    f = w_gate.shape[1]
    slots = 16 * CAP
    half = width // 2
    c = lax.axis_index("c")
    x = lax.axis_index("x")
    cs = jnp.reshape(c, (1,)).astype(jnp.int32)
    others = 1 - cs

    z, y = lax.axis_index("z"), lax.axis_index("y")
    side = x % 2

    piece = lambda k: pl.BlockSpec((rows, 512), lambda i, ar: (0, ar[k]))
    flat = lambda v: pl.BlockSpec(v.shape, lambda i, ar: (0, 0))
    ids, wts = expert_ids.T, route_weights.T
    own = pl.pallas_call(
        pack_kernel,
        grid_spec=prefetched(
            (1,),
            [flat(ids), flat(wts)] + [piece(k) for k in range(6)],
            pl.BlockSpec((rows, 3200), lambda i, ar: (0, 0)),
        ),
        out_shape=like((rows, 3200)),
        cost_estimate=cost(1e7, 2e6),
        name="pack",
    )(
        jnp.stack([2 * k + c for k in (2 * side, 2 * side + 1, 0, 1, 2, 3)]).astype(jnp.int32),
        *(ids, wts, tokens, tokens, grad_out, grad_out, grad_out, grad_out),
    )

    strip = (2, f, 512)
    outgoing = pl.pallas_call(
        outgoing_kernel,
        grid_spec=prefetched(
            (4,),
            [pl.BlockSpec(strip, lambda j, cr: (0, 0, 2 * j + 1 - cr[0]))] * 3,
            pl.BlockSpec((6, f, 512), lambda j, cr: (0, 0, j)),
        ),
        out_shape=like((6, f, half)),
        cost_estimate=cost(0, 9.4e6),
        name="outgoing",
    )(cs, w_gate, w_up, w_down)

    up, down = hop(own, first(1)), hop(own, first(-1))
    up, down, outgoing = together(up, down, outgoing)
    far0, far1, incoming = hop(up[:64], first(1)), hop(down[64:], first(-1)), swap(outgoing)
    far0, far1, incoming = together(far0, far1, incoming)
    far = jnp.concatenate([far0, far1], axis=0)
    line = [own, up, down, far]
    xg = jnp.stack([v[:, :1152] for v in line])
    gg = jnp.stack([v[:, 1152:] for v in line])
    wgu, wd = pl.pallas_call(
        assemble_kernel,
        grid_spec=prefetched(
            (4,),
            [pl.BlockSpec(strip, lambda j, cr: (0, 0, 2 * j + cr[0]))] * 3
            + [pl.BlockSpec((6, f, 512), lambda j, cr: (0, 0, j))],
            [
                pl.BlockSpec((2, 4 * f, 512), lambda j, cr: (0, 0, j)),
                pl.BlockSpec((2, 2 * f, 512), lambda j, cr: (0, 0, j)),
            ],
        ),
        out_shape=(like((2, 4 * f, half)), like((2, 2 * f, half))),
        compiler_params=params(24),
        cost_estimate=cost(0, 19e6),
        name="assemble",
    )(cs, w_gate, w_up, w_down, incoming)
    xm, xr, xg_far = hop(xg, second(1)), hop(xg, second(-1)), hop(xg, along)
    gg, xm, xr, xg_far, wgu, wd = together(gg, xm, xr, xg_far, wgu, wd)
    gm, gr = hop(gg, second(1)), hop(gg, second(-1))
    xd0, xd1 = hop(xm[:2], second(1)), hop(xr[2:], second(-1))
    xm_far = hop(xm, along)

    offsets = (0, -1, 1, 2)
    table = []
    for b in offsets:
        for a in offsets:
            oz, oy = jnp.where(c == 0, a, b), jnp.where(c == 0, b, a)
            table.append((z + oz + 4) % 4 * 4 + (y + oy + 4) % 4)
    info = jnp.stack([2 * (z * 4 + y), side] + table).astype(jnp.int32)

    def select(kernel, start, near, other, into, skip=0):
        is_x = kernel is select_x_kernel
        if is_x:
            specs = [pl.BlockSpec((1, rows, 1152), lambda i, fo: (i, 0, 0))] * 2
        else:
            specs = [
                pl.BlockSpec((1, rows, 128), lambda i, fo: (i + skip, 0, 8)),
                pl.BlockSpec((1, rows, half), lambda i, fo: (i, 0, 0)),
            ]
        n = other.shape[0]
        return pl.pallas_call(
            kernel,
            grid_spec=prefetched(
                (n,),
                specs + [pl.BlockSpec(memory_space=pl.ANY)] * len(into),
                pl.BlockSpec((2, CAP, half), lambda i, fo: (0, fo[2 + start + i], 0)),
                [pltpu.VMEM((rows, rows), F32)],
            ),
            out_shape=like((2, slots, half)),
            input_output_aliases={3: 0} if into else {},
            compiler_params=params(24),
            cost_estimate=cost(2 * n * 2 * CAP * rows * half, n * 1.4e6),
            name="select",
        )(info, near, other, *into)

    xs = select(select_x_kernel, 0, xg, xg_far, [])
    gs = select(select_g_kernel, 0, xg, gg, [])
    xm_far, xr_go, xs, gs = together(xm_far, xr, xs, gs)
    xr_far = hop(xr_go, along)
    xs = select(select_x_kernel, 4, xm, xm_far, [xs])
    gm, gr, xd0, xd1, xr_far, xs = together(gm, gr, xd0, xd1, xr_far, xs)
    gd0, gd1 = hop(gm[:2], second(1)), hop(gr[2:], second(-1))
    xd = jnp.concatenate([xd0, xd1], axis=0)
    xd_far = hop(xd, along)
    gs = select(select_g_kernel, 4, xm, gm, [gs])
    xs = select(select_x_kernel, 8, xr, xr_far, [xs])
    gs = select(select_g_kernel, 8, xr, gr, [gs])
    xs = select(select_x_kernel, 12, xd, xd_far, [xs])
    def hidden(which, v, w, chunk):
        n = w.shape[1]
        return pl.pallas_call(
            hidden_kernel,
            grid_spec=prefetched(
                (n // chunk,),
                [
                    pl.BlockSpec((1, slots, half), lambda j, er: (er[0], 0, 0)),
                    pl.BlockSpec((1, chunk, half), lambda j, er: (er[0], j, 0)),
                ],
                pl.BlockSpec((slots, chunk), lambda j, er: (0, j)),
            ),
            out_shape=like((slots, n), F32),
            compiler_params=params(24),
            cost_estimate=cost(2 * slots * half * n, 9e6),
            name="hidden",
        )(which, v, w)

    pre_out = hidden(others, xs, wgu, 4 * f)
    gd0, gd1, gs, pre_out = together(gd0, gd1, gs, pre_out)
    pre_in = swap(pre_out)
    gs = select(select_g_kernel, 12, xd, gd0, [gs])
    gs = select(select_g_kernel, 14, xd, gd1, [gs], 2)
    dh_out = hidden(others, gs, wd, 2 * f)
    xs, dh_out = together(xs, dh_out)
    dh_in = swap(dh_out)
    pre = hidden(cs, xs, wgu, 4 * f)
    column = lambda k: pl.BlockSpec((slots, 2 * f), lambda j, er: (0, k))
    mine = pl.pallas_call(
        act_kernel,
        grid_spec=prefetched(
            (1,),
            [
                pl.BlockSpec((1, slots, half), lambda j, er: (er[0], 0, 0)),
                pl.BlockSpec((1, 2 * f, half), lambda j, er: (er[0], j, 0)),
                column(0),
                column(0),
                column(0),
                column(1),
                column(1),
            ],
            pl.BlockSpec((slots, 6 * f), lambda j, er: (0, 0)),
        ),
        out_shape=like((slots, 6 * f)),
        compiler_params=params(24),
        cost_estimate=cost(2 * slots * half * 2 * f, 9e6),
        name="act",
    )(cs, gs, wd, dh_in, pre, pre_in, pre, pre_in)
    theirs = swap(mine)

    def partial(kernel, which, ad):
        scratch = []
        if kernel is by_x_kernel:
            shape = like((4, slots, 512))
            out = pl.BlockSpec((1, slots, 512), lambda j, er: (lax.rem(j - er[1] + 4, 4), 0, 0))
        else:
            shape = pltpu.HBM((16, CAP, half), BF)
            out = pl.BlockSpec(memory_space=pltpu.HBM)
            scratch = [pltpu.VMEM((2, 16, CAP, 512), BF), pltpu.SemaphoreType.DMA((2,))]
        return pl.pallas_call(
            kernel,
            grid_spec=prefetched(
                (4,), [VMEM, pl.BlockSpec((1, 4 * f, 512), lambda j, er: (er[0], 0, j))], out, scratch
            ),
            out_shape=shape,
            compiler_params=params(24),
            cost_estimate=cost(2 * slots * half * 4 * f, 8e6),
            name="partial",
        )(jnp.concatenate([which, xx]), ad, wgu)

    shift = lambda v, k: lax.ppermute(v, "x", [(i, (i + k) % 4) for i in range(4)])
    xx = jnp.reshape(x, (1,)).astype(jnp.int32)
    by_block = partial(by_block_kernel, cs, mine)
    row_sums = lax.all_to_all(by_block, ZY, split_axis=0, concat_axis=0, tiled=True)
    by_block, theirs = together(by_block, theirs)
    ring = partial(by_x_kernel, others, theirs)
    ring, mine, theirs = together(ring, mine, theirs)
    r1, r2, r3 = shift(ring[1], 1), shift(ring[2], 2), shift(ring[3], -1)

    pick = lambda i, cr: jnp.where(i == 0, cr[0], 1 - cr[0])
    gg, gu, gd, send = pl.pallas_call(
        weight_kernel,
        grid_spec=prefetched(
            (2, 4),
            [
                VMEM,
                VMEM,
                pl.BlockSpec((1, slots, 512), lambda i, j, cr: (pick(i, cr), 0, j)),
                pl.BlockSpec((1, slots, 512), lambda i, j, cr: (pick(i, cr), 0, j)),
            ],
            [pl.BlockSpec((1, f, 512), lambda i, j, cr: (pick(i, cr), 0, 2 * j + cr[0]))] * 3
            + [pl.BlockSpec((1, 3, f, 512), lambda i, j, cr: (pick(i, cr), 0, 0, j))],
            [pltpu.VMEM((6 * f, slots), BF)],
        ),
        out_shape=[like((2, f, width))] * 3 + [like((2, 3, f, half))],
        compiler_params=params(58),
        cost_estimate=cost(4 * slots * half * 6 * f, 24e6),
        name="weights",
    )(cs, mine, theirs, xs, gs)
    r1, r2, r3, gg, gu, gd, send = together(r1, r2, r3, gg, gu, gd, send)
    kept = sum(v.astype(F32) for v in (ring[0], r1, r2, r3)).astype(BF)
    kept = kept.reshape(16, CAP, 512)
    row_sums, kept, gg, gu, gd, send = together(row_sums, kept, gg, gu, gd, send)
    returned = lax.all_to_all(kept, ZY, split_axis=0, concat_axis=0, tiled=True)
    strips = pl.BlockSpec(strip, lambda j, cr: (0, 0, 2 * j + 1 - cr[0]))
    grads = pl.pallas_call(
        settle_kernel,
        grid_spec=prefetched(
            (4,),
            [pl.BlockSpec((2, 3, f, 512), lambda j, cr: (0, 0, 0, j))] + [pl.BlockSpec(memory_space=pl.ANY)] * 3,
            [strips] * 3,
        ),
        out_shape=[like((2, f, width))] * 3,
        input_output_aliases={2: 0, 3: 1, 4: 2},
        cost_estimate=cost(0, 9.4e6),
        name="settle",
    )(cs, swap(send), gg, gu, gd)

    cx = jnp.concatenate([cs, xx])
    sums = pl.pallas_call(
        rows_kernel,
        out_shape=like((4, rows, 512)),
        in_specs=[SMEM, VMEM, VMEM],
        out_specs=VMEM,
        compiler_params=params(24),
        cost_estimate=cost(1e9, 6.5e6),
        name="rows",
    )(cx, own, row_sums)
    s1, s2, s3 = shift(sums[1], 1), shift(sums[2], 2), shift(sums[3], -1)
    s1, s2, s3, *grads = together(s1, s2, s3, *grads)
    grad_tokens = pl.pallas_call(
        combine_kernel,
        out_shape=like((rows, 512)),
        in_specs=[SMEM] + [VMEM] * 6,
        out_specs=VMEM,
        compiler_params=params(24),
        cost_estimate=cost(1e9, 6.5e6),
        name="combine",
    )(cx, own, returned, sums[0], s1, s2, s3)
    return (grad_tokens, *grads)


def solution(mesh):
    fine = Mesh(mesh.devices.reshape(4, 4, 4, 2), ("z", "y", "x", "c"))
    rows = P(ZY, None)
    weights = P(ZY, ("x", "c"), None)
    return jax.shard_map(
        shards,
        mesh=fine,
        in_specs=(rows, rows, rows, rows, weights, weights, weights),
        out_specs=(P(ZY, ("x", "c")), weights, weights, weights),
        check_vma=False,
    )
```

```python
import jax
import jax.numpy as jnp
from jax import lax
from jax.experimental import pallas as pl
from jax.experimental.pallas import tpu as pltpu
from jax.sharding import Mesh
from jax.sharding import PartitionSpec as P

BF = jnp.bfloat16
F32 = jnp.float32
CAP = 48
ZY = ("z", "y")
ZYX = ("z", "y", "x")
VMEM = pl.BlockSpec(memory_space=pltpu.VMEM)
SMEM = pl.BlockSpec(memory_space=pltpu.SMEM)
SWAP = [(0, 1), (1, 0)]


def params(mib):
    return pltpu.CompilerParams(vmem_limit_bytes=mib * 1024 * 1024)


def cost(flops, nbytes):
    return pl.CostEstimate(flops=int(flops / 1e3), bytes_accessed=int(nbytes / 1e3), transcendentals=0)


def nt(a, b):
    return lax.dot_general(a, b, (((1,), (1,)), ((), ())), preferred_element_type=F32)


def mm(a, b):
    return jnp.dot(a, b, preferred_element_type=F32)


def swap(v):
    return lax.ppermute(v, "c", SWAP)


def pairs(to):
    spot = lambda z, y, x, c: ((z % 4 * 4 + y % 4) * 4 + x % 4) * 2 + c
    places = [(z, y, x, c) for z in range(4) for y in range(4) for x in range(4) for c in range(2)]
    return [(spot(*p), spot(*to(*p))) for p in places]


def first(s):
    return pairs(lambda z, y, x, c: (z + s, y, x, c) if c == 0 else (z, y + s, x, c))


def second(s):
    return pairs(lambda z, y, x, c: (z, y + s, x, c) if c == 0 else (z + s, y, x, c))


along = pairs(lambda z, y, x, c: (z, y, x + 1 if c == 0 else x - 1, c))


def hop(v, to):
    return lax.ppermute(v, ("z", "y", "x", "c"), to)


def together(*v):
    return lax.optimization_barrier(v)


def like(shape, dtype=BF):
    return jax.ShapeDtypeStruct(shape, dtype)


def prefetched(grid, in_specs, out_specs, scratch=()):
    return pltpu.PrefetchScalarGridSpec(
        num_scalar_prefetch=1, grid=grid, in_specs=in_specs, out_specs=out_specs, scratch_shapes=list(scratch)
    )


def pack_kernel(at_ref, ids_ref, wts_ref, t0, t1, g0, g1, g2, g3, out_ref):
    top, rows = ids_ref.shape
    expert = lax.broadcasted_iota(jnp.int32, (32, rows), 0)
    hit = jnp.zeros((32, rows), F32)
    wt = jnp.zeros((32, rows), F32)
    for k in range(top):
        same = ids_ref[k : k + 1, :] == expert
        hit = hit + same.astype(F32)
        wt = wt + jnp.where(same, wts_ref[k : k + 1, :], 0.0)
    r = lax.broadcasted_iota(jnp.int32, (rows, rows), 0)
    q = lax.broadcasted_iota(jnp.int32, (rows, rows), 1)
    before = mm(hit.astype(BF), (r < q).astype(BF))
    pos = jnp.where(hit > 0.5, before, -1.0)
    high = wt.astype(BF)
    rest = wt - high.astype(F32)
    mid = rest.astype(BF)
    low = (rest - mid.astype(F32)).astype(BF)
    out_ref[:, 0:512] = t0[...]
    out_ref[:, 512:1024] = t1[...]
    out_ref[:, 1024:1152] = jnp.concatenate([pos.astype(BF), high, mid, low], axis=0)
    for i, ref in enumerate((g0, g1, g2, g3)):
        out_ref[:, 1152 + i * 512 : 1664 + i * 512] = ref[...]


def chosen(row):
    p = lax.broadcasted_iota(jnp.int32, (CAP, row.shape[1]), 0).astype(F32)
    return row == p


def outgoing_kernel(c_ref, g_ref, u_ref, d_ref, out_ref):
    out_ref[0:2] = g_ref[...]
    out_ref[2:4] = u_ref[...]
    out_ref[4:6] = d_ref[...]


def assemble_kernel(c_ref, g_ref, u_ref, d_ref, in_ref, wgu_ref, wd_ref):
    f = g_ref.shape[1]

    def place(low, high):
        for e in range(2):
            wgu_ref[e, low : low + f] = g_ref[e]
            wgu_ref[e, high : high + f] = in_ref[e]
            wgu_ref[e, 2 * f + low : 3 * f + low] = u_ref[e]
            wgu_ref[e, 2 * f + high : 3 * f + high] = in_ref[2 + e]
            wd_ref[e, low : low + f] = d_ref[e]
            wd_ref[e, high : high + f] = in_ref[4 + e]

    @pl.when(c_ref[0] == 0)
    def _():
        place(0, f)

    @pl.when(c_ref[0] == 1)
    def _():
        place(f, 0)


def picked(info_ref, meta, held):
    held[...] = meta.astype(F32)
    picks, scales = [], []
    for k in range(2):
        row = info_ref[0] + k
        pick = chosen(held[pl.ds(row, 1), :])
        wt = held[pl.ds(32 + row, 1), :] + held[pl.ds(64 + row, 1), :] + held[pl.ds(96 + row, 1), :]
        picks.append(pick.astype(F32))
        scales.append(jnp.sum(jnp.where(pick, wt, 0.0), axis=1, keepdims=True))
    return jnp.concatenate(picks, axis=0).astype(BF), jnp.concatenate(scales, axis=0)


def select_x_kernel(info_ref, near_ref, far_ref, *rest):
    out_ref, held = rest[-2:]
    w = out_ref.shape[2] // 2
    pick, _ = picked(info_ref, near_ref[0, :, w:], held)
    for i, ref in enumerate((near_ref, far_ref)):
        got = mm(pick, ref[0, :, 0:w]).astype(BF)
        side = info_ref[1] if i == 0 else 1 - info_ref[1]
        cols = pl.ds(pl.multiple_of(side * w, w), w)
        out_ref[0, :, cols] = got[0:CAP]
        out_ref[1, :, cols] = got[CAP:]


def select_g_kernel(info_ref, near_ref, g_ref, *rest):
    out_ref, held = rest[-2:]
    pick, scale = picked(info_ref, near_ref[0], held)
    got = (mm(pick, g_ref[0]) * scale).astype(BF)
    out_ref[0] = got[0:CAP]
    out_ref[1] = got[CAP:]


def hidden_kernel(e_ref, v_ref, w_ref, out_ref):
    out_ref[...] = nt(v_ref[0], w_ref[0])


def act_kernel(e_ref, v_ref, w_ref, d_ref, g0_ref, g1_ref, u0_ref, u1_ref, out_ref):
    n = out_ref.shape[1] // 3
    d = nt(v_ref[0], w_ref[0]) + d_ref[...]
    gate, up = g0_ref[...] + g1_ref[...], u0_ref[...] + u1_ref[...]
    sig = jax.nn.sigmoid(gate)
    silu = gate * sig
    outs = (d * up * sig * (1.0 + gate * (1.0 - sig)), d * silu, silu * up)
    for i, value in enumerate(outs):
        out_ref[:, i * n : (i + 1) * n] = value.astype(BF)


def by_x_kernel(e_ref, ad_ref, wgu_ref, out_ref):
    out_ref[0] = mm(ad_ref[:, 0 : wgu_ref.shape[1]], wgu_ref[0]).astype(BF)


def by_block_kernel(e_ref, ad_ref, wgu_ref, out_ref, stage, sems):
    step = pl.program_id(0)

    def leaving(j, slot):
        cols = pl.ds(pl.multiple_of(j * 1024, 1024), 1024)
        return pltpu.make_async_copy(stage.at[slot], out_ref.at[:, :, cols], sems.at[slot])

    got = mm(ad_ref[:, 0 : wgu_ref.shape[1]], wgu_ref[0]).astype(BF)
    stage[step] = got.reshape(stage.shape[1:])
    leaving(step, step).start()

    @pl.when(step == 1)
    def _():
        leaving(0, 0).wait()
        leaving(1, 1).wait()


def weight_kernel(c_ref, mine_ref, theirs_ref, xs_ref, gs_ref, gg_ref, gu_ref, gd_ref, send_ref, dt):
    f = gg_ref.shape[1]
    first = pl.program_id(1) == 0

    @pl.when(first & (pl.program_id(0) == 0))
    def _():
        dt[...] = mine_ref[...].astype(F32).T.astype(BF)

    @pl.when(first & (pl.program_id(0) == 1))
    def _():
        dt[...] = theirs_ref[...].astype(F32).T.astype(BF)

    c = c_ref[0]
    outs = (gg_ref, gu_ref, gd_ref)
    for i in range(3):
        rows = xs_ref if i < 2 else gs_ref
        keep = pl.ds(pl.multiple_of(2 * f * i + f * c, f), f)
        away = pl.ds(pl.multiple_of(2 * f * i + f * (1 - c), f), f)
        outs[i][0] = mm(dt[keep, :], rows[0]).astype(BF)
        send_ref[0, i] = mm(dt[away, :], rows[0]).astype(BF)


def settle_kernel(c_ref, in_ref, a_ref, b_ref, d_ref, gg_ref, gu_ref, gd_ref):
    for e in range(2):
        gg_ref[e] = in_ref[e, 0]
        gu_ref[e] = in_ref[e, 1]
        gd_ref[e] = in_ref[e, 2]


def gathering(parity, pw_ref):
    low = parity == 0
    places = pw_ref[0:32, 1024:1152].astype(F32)
    picks = []
    for e in range(16):
        row = jnp.where(low, places[2 * e : 2 * e + 1], places[2 * e + 1 : 2 * e + 2])
        picks.append(chosen(row).astype(F32))
    return jnp.concatenate(picks, axis=0).T.astype(BF)


def rows_kernel(c_ref, pw_ref, ret_ref, out_ref):
    total = mm(gathering(c_ref[0], pw_ref), ret_ref[...].reshape(16 * CAP, 2048)).astype(BF)
    for j in range(4):
        out_ref[lax.rem(j - c_ref[1] + 4, 4)] = total[:, j * 512 : (j + 1) * 512]


def combine_kernel(c_ref, pw_ref, ret_ref, a_ref, b_ref, d_ref, e_ref, out_ref):
    total = mm(gathering(1 - c_ref[0], pw_ref), ret_ref[...].reshape(16 * CAP, 512))
    for ref in (a_ref, b_ref, d_ref, e_ref):
        total = total + ref[...].astype(F32)
    out_ref[...] = total.astype(BF)


def shards(tokens, expert_ids, route_weights, grad_out, w_gate, w_up, w_down):
    rows, width = tokens.shape
    f = w_gate.shape[1]
    slots = 16 * CAP
    half = width // 2
    c = lax.axis_index("c")
    x = lax.axis_index("x")
    cs = jnp.reshape(c, (1,)).astype(jnp.int32)
    others = 1 - cs

    z, y = lax.axis_index("z"), lax.axis_index("y")
    side = x % 2

    piece = lambda k: pl.BlockSpec((rows, 512), lambda i, ar: (0, ar[k]))
    flat = lambda v: pl.BlockSpec(v.shape, lambda i, ar: (0, 0))
    ids, wts = expert_ids.T, route_weights.T
    own = pl.pallas_call(
        pack_kernel,
        grid_spec=prefetched(
            (1,),
            [flat(ids), flat(wts)] + [piece(k) for k in range(6)],
            pl.BlockSpec((rows, 3200), lambda i, ar: (0, 0)),
        ),
        out_shape=like((rows, 3200)),
        cost_estimate=cost(1e7, 2e6),
        name="pack",
    )(
        jnp.stack([2 * k + c for k in (2 * side, 2 * side + 1, 0, 1, 2, 3)]).astype(jnp.int32),
        *(ids, wts, tokens, tokens, grad_out, grad_out, grad_out, grad_out),
    )

    strip = (2, f, 512)
    outgoing = pl.pallas_call(
        outgoing_kernel,
        grid_spec=prefetched(
            (4,),
            [pl.BlockSpec(strip, lambda j, cr: (0, 0, 2 * j + 1 - cr[0]))] * 3,
            pl.BlockSpec((6, f, 512), lambda j, cr: (0, 0, j)),
        ),
        out_shape=like((6, f, half)),
        cost_estimate=cost(0, 9.4e6),
        name="outgoing",
    )(cs, w_gate, w_up, w_down)

    up, down = hop(own, first(1)), hop(own, first(-1))
    up, down, outgoing = together(up, down, outgoing)
    far0, far1, incoming = hop(up[:64], first(1)), hop(down[64:], first(-1)), swap(outgoing)
    far0, far1, incoming = together(far0, far1, incoming)
    far = jnp.concatenate([far0, far1], axis=0)
    line = [own, up, down, far]
    xg = jnp.stack([v[:, :1152] for v in line])
    gg = jnp.stack([v[:, 1152:] for v in line])
    wgu, wd = pl.pallas_call(
        assemble_kernel,
        grid_spec=prefetched(
            (4,),
            [pl.BlockSpec(strip, lambda j, cr: (0, 0, 2 * j + cr[0]))] * 3
            + [pl.BlockSpec((6, f, 512), lambda j, cr: (0, 0, j))],
            [
                pl.BlockSpec((2, 4 * f, 512), lambda j, cr: (0, 0, j)),
                pl.BlockSpec((2, 2 * f, 512), lambda j, cr: (0, 0, j)),
            ],
        ),
        out_shape=(like((2, 4 * f, half)), like((2, 2 * f, half))),
        compiler_params=params(24),
        cost_estimate=cost(0, 19e6),
        name="assemble",
    )(cs, w_gate, w_up, w_down, incoming)
    xm, xr, xg_far = hop(xg, second(1)), hop(xg, second(-1)), hop(xg, along)
    gg, xm, xr, xg_far, wgu, wd = together(gg, xm, xr, xg_far, wgu, wd)
    gm, gr = hop(gg, second(1)), hop(gg, second(-1))
    xd0, xd1 = hop(xm[:2], second(1)), hop(xr[2:], second(-1))
    xm_far = hop(xm, along)

    offsets = (0, -1, 1, 2)
    table = []
    for b in offsets:
        for a in offsets:
            oz, oy = jnp.where(c == 0, a, b), jnp.where(c == 0, b, a)
            table.append((z + oz + 4) % 4 * 4 + (y + oy + 4) % 4)
    info = jnp.stack([2 * (z * 4 + y), side] + table).astype(jnp.int32)

    def select(kernel, start, near, other, into, skip=0):
        is_x = kernel is select_x_kernel
        if is_x:
            specs = [pl.BlockSpec((1, rows, 1152), lambda i, fo: (i, 0, 0))] * 2
        else:
            specs = [
                pl.BlockSpec((1, rows, 128), lambda i, fo: (i + skip, 0, 8)),
                pl.BlockSpec((1, rows, half), lambda i, fo: (i, 0, 0)),
            ]
        n = other.shape[0]
        return pl.pallas_call(
            kernel,
            grid_spec=prefetched(
                (n,),
                specs + [pl.BlockSpec(memory_space=pl.ANY)] * len(into),
                pl.BlockSpec((2, CAP, half), lambda i, fo: (0, fo[2 + start + i], 0)),
                [pltpu.VMEM((rows, rows), F32)],
            ),
            out_shape=like((2, slots, half)),
            input_output_aliases={3: 0} if into else {},
            compiler_params=params(24),
            cost_estimate=cost(2 * n * 2 * CAP * rows * half, n * 1.4e6),
            name="select",
        )(info, near, other, *into)

    xs = select(select_x_kernel, 0, xg, xg_far, [])
    gs = select(select_g_kernel, 0, xg, gg, [])
    xm_far, xr_go, xs, gs = together(xm_far, xr, xs, gs)
    xr_far = hop(xr_go, along)
    xs = select(select_x_kernel, 4, xm, xm_far, [xs])
    gm, gr, xd0, xd1, xr_far, xs = together(gm, gr, xd0, xd1, xr_far, xs)
    gd0, gd1 = hop(gm[:2], second(1)), hop(gr[2:], second(-1))
    xd = jnp.concatenate([xd0, xd1], axis=0)
    xd_far = hop(xd, along)
    gs = select(select_g_kernel, 4, xm, gm, [gs])
    xs = select(select_x_kernel, 8, xr, xr_far, [xs])
    gs = select(select_g_kernel, 8, xr, gr, [gs])
    xs = select(select_x_kernel, 12, xd, xd_far, [xs])
    def hidden(which, v, w, chunk):
        n = w.shape[1]
        return pl.pallas_call(
            hidden_kernel,
            grid_spec=prefetched(
                (n // chunk,),
                [
                    pl.BlockSpec((1, slots, half), lambda j, er: (er[0], 0, 0)),
                    pl.BlockSpec((1, chunk, half), lambda j, er: (er[0], j, 0)),
                ],
                pl.BlockSpec((slots, chunk), lambda j, er: (0, j)),
            ),
            out_shape=like((slots, n), F32),
            compiler_params=params(24),
            cost_estimate=cost(2 * slots * half * n, 9e6),
            name="hidden",
        )(which, v, w)

    pre_out = hidden(others, xs, wgu, 4 * f)
    gd0, gd1, gs, pre_out = together(gd0, gd1, gs, pre_out)
    pre_in = swap(pre_out)
    gs = select(select_g_kernel, 12, xd, gd0, [gs])
    gs = select(select_g_kernel, 14, xd, gd1, [gs], 2)
    dh_out = hidden(others, gs, wd, 2 * f)
    xs, dh_out = together(xs, dh_out)
    dh_in = swap(dh_out)
    pre = hidden(cs, xs, wgu, 4 * f)
    column = lambda k: pl.BlockSpec((slots, 2 * f), lambda j, er: (0, k))
    mine = pl.pallas_call(
        act_kernel,
        grid_spec=prefetched(
            (1,),
            [
                pl.BlockSpec((1, slots, half), lambda j, er: (er[0], 0, 0)),
                pl.BlockSpec((1, 2 * f, half), lambda j, er: (er[0], j, 0)),
                column(0),
                column(0),
                column(0),
                column(1),
                column(1),
            ],
            pl.BlockSpec((slots, 6 * f), lambda j, er: (0, 0)),
        ),
        out_shape=like((slots, 6 * f)),
        compiler_params=params(24),
        cost_estimate=cost(2 * slots * half * 2 * f, 9e6),
        name="act",
    )(cs, gs, wd, dh_in, pre, pre_in, pre, pre_in)
    theirs = swap(mine)

    def partial(kernel, which, ad):
        scratch = []
        wide = 512 if kernel is by_x_kernel else 1024
        if kernel is by_x_kernel:
            shape = like((4, slots, 512))
            out = pl.BlockSpec((1, slots, 512), lambda j, er: (lax.rem(j - er[1] + 4, 4), 0, 0))
        else:
            shape = pltpu.HBM((16, CAP, half), BF)
            out = pl.BlockSpec(memory_space=pltpu.HBM)
            scratch = [pltpu.VMEM((2, 16, CAP, 1024), BF), pltpu.SemaphoreType.DMA((2,))]
        return pl.pallas_call(
            kernel,
            grid_spec=prefetched(
                (half // wide,), [VMEM, pl.BlockSpec((1, 4 * f, wide), lambda j, er: (er[0], 0, j))], out, scratch
            ),
            out_shape=shape,
            compiler_params=params(24),
            cost_estimate=cost(2 * slots * half * 4 * f, 8e6),
            name="partial",
        )(jnp.concatenate([which, xx]), ad, wgu)

    shift = lambda v, k: lax.ppermute(v, "x", [(i, (i + k) % 4) for i in range(4)])
    xx = jnp.reshape(x, (1,)).astype(jnp.int32)
    by_block = partial(by_block_kernel, cs, mine)
    row_sums = lax.all_to_all(by_block, ZY, split_axis=0, concat_axis=0, tiled=True)
    by_block, theirs = together(by_block, theirs)
    ring = partial(by_x_kernel, others, theirs)
    ring, mine, theirs = together(ring, mine, theirs)
    r1, r2, r3 = shift(ring[1], 1), shift(ring[2], 2), shift(ring[3], -1)

    pick = lambda i, cr: jnp.where(i == 0, cr[0], 1 - cr[0])
    gg, gu, gd, send = pl.pallas_call(
        weight_kernel,
        grid_spec=prefetched(
            (2, 4),
            [
                VMEM,
                VMEM,
                pl.BlockSpec((1, slots, 512), lambda i, j, cr: (pick(i, cr), 0, j)),
                pl.BlockSpec((1, slots, 512), lambda i, j, cr: (pick(i, cr), 0, j)),
            ],
            [pl.BlockSpec((1, f, 512), lambda i, j, cr: (pick(i, cr), 0, 2 * j + cr[0]))] * 3
            + [pl.BlockSpec((1, 3, f, 512), lambda i, j, cr: (pick(i, cr), 0, 0, j))],
            [pltpu.VMEM((6 * f, slots), BF)],
        ),
        out_shape=[like((2, f, width))] * 3 + [like((2, 3, f, half))],
        compiler_params=params(58),
        cost_estimate=cost(4 * slots * half * 6 * f, 24e6),
        name="weights",
    )(cs, mine, theirs, xs, gs)
    r1, r2, r3, gg, gu, gd, send = together(r1, r2, r3, gg, gu, gd, send)
    kept = sum(v.astype(F32) for v in (ring[0], r1, r2, r3)).astype(BF)
    kept = kept.reshape(16, CAP, 512)
    row_sums, kept, gg, gu, gd, send = together(row_sums, kept, gg, gu, gd, send)
    returned = lax.all_to_all(kept, ZY, split_axis=0, concat_axis=0, tiled=True)
    strips = pl.BlockSpec(strip, lambda j, cr: (0, 0, 2 * j + 1 - cr[0]))
    grads = pl.pallas_call(
        settle_kernel,
        grid_spec=prefetched(
            (4,),
            [pl.BlockSpec((2, 3, f, 512), lambda j, cr: (0, 0, 0, j))] + [pl.BlockSpec(memory_space=pl.ANY)] * 3,
            [strips] * 3,
        ),
        out_shape=[like((2, f, width))] * 3,
        input_output_aliases={2: 0, 3: 1, 4: 2},
        cost_estimate=cost(0, 9.4e6),
        name="settle",
    )(cs, swap(send), gg, gu, gd)

    cx = jnp.concatenate([cs, xx])
    sums = pl.pallas_call(
        rows_kernel,
        out_shape=like((4, rows, 512)),
        in_specs=[SMEM, VMEM, VMEM],
        out_specs=VMEM,
        compiler_params=params(24),
        cost_estimate=cost(1e9, 6.5e6),
        name="rows",
    )(cx, own, row_sums)
    s1, s2, s3 = shift(sums[1], 1), shift(sums[2], 2), shift(sums[3], -1)
    s1, s2, s3, *grads = together(s1, s2, s3, *grads)
    grad_tokens = pl.pallas_call(
        combine_kernel,
        out_shape=like((rows, 512)),
        in_specs=[SMEM] + [VMEM] * 6,
        out_specs=VMEM,
        compiler_params=params(24),
        cost_estimate=cost(1e9, 6.5e6),
        name="combine",
    )(cx, own, returned, sums[0], s1, s2, s3)
    return (grad_tokens, *grads)


def solution(mesh):
    fine = Mesh(mesh.devices.reshape(4, 4, 4, 2), ("z", "y", "x", "c"))
    rows = P(ZY, None)
    weights = P(ZY, ("x", "c"), None)
    return jax.shard_map(
        shards,
        mesh=fine,
        in_specs=(rows, rows, rows, rows, weights, weights, weights),
        out_specs=(P(ZY, ("x", "c")), weights, weights, weights),
        check_vma=False,
    )
```
